32 devices in a mesh: dp: 4 (over y, core), seq: 8 (over z, x).
Axes of the slice: x: 2, y: 2, z: 4, core: 2. Of those that a mesh axis runs over, the one named last changes fastest.
Arguments:
- hidden_in: bfloat16 [8, 1024, 1408], P('dp', 'seq'), may hold values from -6 to 6
- skip_in: bfloat16 [8, 1024, 1408], P('dp', 'seq'), may hold values from -6 to 6
- text_states: bfloat16 [8, 333, 1024], P('dp', None, 'seq'), may hold values from -6 to 6
- timesteps: int32 [8], P('dp'), may hold values from 0 to 999
- positions: int32 [8, 2, 1024], P('dp', None, 'seq'), may hold values from 0 to 63, as said below
- cotangent: bfloat16 [8, 1024, 1408], P('dp', 'seq'), may hold values from -6 to 6
- skip_gain: float32 [2816], replicated, may hold values from 0.1 to 1.9
- skip_weight: bfloat16 [2816, 1408], P('dp'), may hold values from -0.109375 to 0.109375
- self_norm_gain: float32 [1408], replicated, may hold values from 0.1 to 1.9
- shift_weight: bfloat16 [1408, 1408], P('dp'), may hold values from -0.21875 to 0.21875
- qkv_weight: bfloat16 [1408, 4224], P('dp'), may hold values from -0.15625 to 0.15625
- query_gain: float32 [88], replicated, may hold values from 0.1 to 1.9
- key_gain: float32 [88], replicated, may hold values from 0.1 to 1.9
- self_out_weight: bfloat16 [1408, 1408], P('dp'), may hold values from -6 to 6
- cross_norm_gain: float32 [1408], replicated, may hold values from 0.1 to 1.9
- cross_query_weight: bfloat16 [1408, 1408], P('dp'), may hold values from -0.15625 to 0.15625
- text_kv_weight: bfloat16 [1024, 16, 176], P('dp', 'seq'), may hold values from -0.1875 to 0.1875
- cross_query_gain: float32 [88], replicated, may hold values from 0.1 to 1.9
- cross_key_gain: float32 [88], replicated, may hold values from 0.1 to 1.9
- cross_out_weight: bfloat16 [1408, 1408], P('dp'), may hold values from -3 to 3
- ffn_norm_gain: float32 [1408], replicated, may hold values from 0.1 to 1.9
- ffn_up_weight: bfloat16 [1408, 6144], P('dp'), may hold values from -0.15625 to 0.15625
- ffn_down_weight: bfloat16 [6144, 1408], P('dp'), may hold values from -0.078125 to 0.078125
Outputs:
- block_out: bfloat16 [8, 1024, 1408], P('dp', 'seq')
- hidden_grad: bfloat16 [8, 1024, 1408], P('dp', 'seq')
- skip_grad: bfloat16 [8, 1024, 1408], P('dp', 'seq')
- text_grad: bfloat16 [8, 333, 1024], P('dp', None, 'seq')
- skip_gain_grad: float32 [2816], replicated
- skip_weight_grad: float32 [2816, 1408], P('dp')
- self_norm_gain_grad: float32 [1408], replicated
- shift_weight_grad: float32 [1408, 1408], P('dp')
- qkv_weight_grad: float32 [1408, 4224], P('dp')
- query_gain_grad: float32 [88], replicated
- key_gain_grad: float32 [88], replicated
- self_out_weight_grad: float32 [1408, 1408], P('dp')
- cross_norm_gain_grad: float32 [1408], replicated
- cross_query_weight_grad: float32 [1408, 1408], P('dp')
- text_kv_weight_grad: float32 [1024, 16, 176], P('dp', 'seq')
- cross_query_gain_grad: float32 [88], replicated
- cross_key_gain_grad: float32 [88], replicated
- cross_out_weight_grad: float32 [1408, 1408], P('dp')
- ffn_norm_gain_grad: float32 [1408], replicated
- ffn_up_weight_grad: float32 [1408, 6144], P('dp')
- ffn_down_weight_grad: float32 [6144, 1408], P('dp')
The draws below stay inside these ranges and needn't reach their ends.
Inputs may be any that keep to these rules, and one draw needn't show every extreme that they name: `positions`: each latent's tokens lie in row-major order on a grid of 16, 32 or 64 columns; entry 0 is a token's grid row, entry 1 its column.
All inputs are finite; a program needn't handle non-finite values.
Results may differ from the reference program's by a relative error of at most 0.023.
Values may be sent and summed in bfloat16 or wider, within the bound.
No kernel may reach another device: no remote copies, remote signals or barrier semaphores. Data moves between devices by JAX's collectives and lax.ppermute only.
A program may use at most 320 MiB of HBM per device.

```python
import math
import jax
import jax.numpy as jnp
from jax import lax

H = 16
HD = 88
D = 1408
FF = 6144
C = 1024
M = 333
GRIDW = 32
L = 1024
LATENTS = 8


def draw_positions(key, part):
    key = jax.random.fold_in(key, 7)
    column_pick = jax.random.randint(key, (LATENTS,), 0, 3)
    column_pick = column_pick.at[0].set(0)
    grid_width = jnp.where(column_pick == 0, GRIDW // 2, jnp.where(column_pick == 1, GRIDW, 2 * GRIDW)).astype(jnp.int32)
    token_index = jnp.arange(L, dtype=jnp.int32)
    row_pos = token_index[None, :] // grid_width[:, None]
    col_pos = token_index[None, :] % grid_width[:, None]
    return jnp.stack([row_pos, col_pos], axis=1).astype(jnp.int32)


def set_ends(values, own_key, smallest, high):
    place = [jax.random.randint(jax.random.fold_in(own_key, axis), (), 0, length) for axis, length in enumerate(values.shape)]
    main_axis = values.shape.index(max(values.shape))
    beside = place[:main_axis] + [(place[main_axis] + 1) % values.shape[main_axis]] + place[main_axis + 1:]
    return values.at[tuple(place)].set(smallest).at[tuple(beside)].set(high)


def level_of(key, shape, split, low, largest):
    loudness = 1.0
    for axis_at, blocks in split:
        heights = jax.random.uniform(jax.random.fold_in(jax.random.fold_in(key, 6), axis_at), (blocks,), jnp.float32, low / len(split), largest / len(split))
        loudness = loudness * jnp.repeat(jnp.exp(heights), shape[axis_at] // blocks).reshape((-1,) + (1,) * (len(shape) - 1 - axis_at))
    return loudness


def normal_values(rng, dims, width, most, pieces=(), held_as=jnp.bfloat16):
    entries = width * jax.random.normal(rng, dims, jnp.float32)
    if pieces:
        entries = entries * level_of(rng, dims, pieces, -0.22, 0.18)
    return jnp.clip(entries, -most, most).astype(held_as)


def setup_inputs(seed: int = 0) -> dict:
    arg_keys = jax.random.split(jax.random.key(seed), 24)
    return {
        "hidden_in": normal_values(arg_keys[0], (LATENTS, L, D), 1.0, 6.0, ((0, 4), (1, 8))),
        "skip_in": normal_values(arg_keys[1], (LATENTS, L, D), 1.0, 6.0, ((0, 4), (1, 8))),
        "text_states": normal_values(arg_keys[2], (LATENTS, M, C), 1.0, 6.0, ((0, 4), (2, 8))),
        "timesteps": set_ends(jax.random.randint(arg_keys[3], (LATENTS,), 0, 1000), jax.random.fold_in(arg_keys[3], 1), 0, 999).astype(jnp.int32),
        "positions": draw_positions(jax.random.fold_in(arg_keys[23], 71), 0),
        "cotangent": normal_values(arg_keys[5], (LATENTS, L, D), 1.0, 6.0, ((0, 4), (1, 8))),
        "skip_gain": jnp.clip(1.0 + 0.18 * jax.random.normal(arg_keys[6], (2 * D,), jnp.float32), 0.1, 1.9),
        "skip_weight": normal_values(arg_keys[7], (2 * D, D), (2 * D) ** -0.5, 0.109375, ((0, 4),)),
        "self_norm_gain": jnp.clip(1.0 + 0.18 * jax.random.normal(arg_keys[8], (D,), jnp.float32), 0.1, 1.9),
        "shift_weight": normal_values(arg_keys[9], (D, D), (D // 2) ** -0.5, 0.21875, ((0, 4),)),
        "qkv_weight": normal_values(arg_keys[10], (D, 3 * D), D ** -0.5, 0.15625, ((0, 4),)),
        "query_gain": jnp.clip(1.0 + 0.18 * jax.random.normal(arg_keys[11], (HD,), jnp.float32), 0.1, 1.9),
        "key_gain": jnp.clip(1.0 + 0.18 * jax.random.normal(arg_keys[12], (HD,), jnp.float32), 0.1, 1.9),
        "self_out_weight": normal_values(arg_keys[13], (D, D), (max(1, D // L)) ** -0.5, 6.0, ((0, 4),)),
        "cross_norm_gain": jnp.clip(1.0 + 0.18 * jax.random.normal(arg_keys[14], (D,), jnp.float32), 0.1, 1.9),
        "cross_query_weight": normal_values(arg_keys[15], (D, D), D ** -0.5, 0.15625, ((0, 4),)),
        "text_kv_weight": normal_values(arg_keys[16], (C, H, 2 * HD), C ** -0.5, 0.1875, ((0, 4), (1, 8))),
        "cross_query_gain": jnp.clip(1.0 + 0.18 * jax.random.normal(arg_keys[17], (HD,), jnp.float32), 0.1, 1.9),
        "cross_key_gain": jnp.clip(1.0 + 0.18 * jax.random.normal(arg_keys[18], (HD,), jnp.float32), 0.1, 1.9),
        "cross_out_weight": normal_values(arg_keys[19], (D, D), (max(1, D // M)) ** -0.5, 3.0, ((0, 4),)),
        "ffn_norm_gain": jnp.clip(1.0 + 0.18 * jax.random.normal(arg_keys[20], (D,), jnp.float32), 0.1, 1.9),
        "ffn_up_weight": normal_values(arg_keys[21], (D, FF), D ** -0.5, 0.15625, ((0, 4),)),
        "ffn_down_weight": normal_values(arg_keys[22], (FF, D), FF ** -0.5, 0.078125, ((0, 4),)),
    }


@jax.custom_vjp
def low(v):
    return lax.optimization_barrier(v.astype(jnp.bfloat16)).astype(jnp.float32)

@jax.custom_vjp
def low_back(v):
    return v

def low_keep(v):
    return (low(v), None)

def low_pass(kept, grad):
    return (grad,)

def back_keep(v):
    return (v, None)

def back_low(kept, grad):
    return (low(grad),)
low.defvjp(low_keep, low_pass)
low_back.defvjp(back_keep, back_low)
norm_eps = 1e-06
highest = lax.Precision.HIGHEST

def layer_norm(tensor, gain_vec):
    center = tensor - lax.optimization_barrier(jnp.mean(tensor, axis=-1, keepdims=True))
    spread = lax.optimization_barrier(jnp.mean(center * center, axis=-1, keepdims=True))
    return center * lax.rsqrt(spread + norm_eps) * gain_vec

def project(left_side, right_side):
    return jnp.einsum('...i,ij->...j', left_side, right_side, precision=highest, preferred_element_type=jnp.float32)

def time_embed(step_ids, embed_width):
    half_width = embed_width // 2
    frequency = jnp.exp(-math.log(10000.0) * jnp.arange(half_width, dtype=jnp.float32) / half_width)
    angles = step_ids.astype(jnp.float32)[:, None] * frequency[None, :]
    return jnp.concatenate([jnp.cos(angles), jnp.sin(angles)], axis=-1)

def rope_tables(grid_pos, head_dim):
    quarter = head_dim // 4
    frequency = jnp.exp(-math.log(10000.0) * jnp.arange(quarter, dtype=jnp.float32) / quarter)
    row_angle = grid_pos[:, 0, :].astype(jnp.float32)[:, :, None, None] * frequency
    col_angle = grid_pos[:, 1, :].astype(jnp.float32)[:, :, None, None] * frequency
    return (jnp.cos(row_angle), jnp.sin(row_angle), jnp.cos(col_angle), jnp.sin(col_angle))

def rotate(tensor, tables):
    cos_row, sin_row, cos_col, sin_col = tables
    quarter = tensor.shape[-1] // 4
    first_part = tensor[..., :quarter]
    second_part = tensor[..., quarter:2 * quarter]
    third_part = tensor[..., 2 * quarter:3 * quarter]
    fourth_part = tensor[..., 3 * quarter:]
    return jnp.concatenate([first_part * cos_row - second_part * sin_row, second_part * cos_row + first_part * sin_row, third_part * cos_col - fourth_part * sin_col, fourth_part * cos_col + third_part * sin_col], axis=-1)

def attend(queries, keys_in, values_in):
    row_count = queries.shape[2]
    row_block = min(512, row_count)
    score_scale = queries.shape[-1] ** (-0.5)
    shaped = queries.reshape(queries.shape[0], queries.shape[1], row_count // row_block, row_block, queries.shape[3])
    shaped = jnp.moveaxis(shaped, 2, 0)

    def one_block(query_part):
        scores = low_back(score_scale * jnp.einsum('ghqe,ghke->ghqk', query_part, keys_in, precision=highest, preferred_element_type=jnp.float32))
        weights = jax.nn.softmax(scores, axis=-1)
        return jnp.einsum('ghqk,ghke->ghqe', low(weights), values_in, precision=highest, preferred_element_type=jnp.float32)
    result = lax.map(jax.checkpoint(one_block), shaped)
    return jnp.moveaxis(result, 0, 2).reshape(queries.shape)

def layer_forward(hidden, skipped, text_rows, shift_embed, tables, skip_gain, skip_weight, self_norm_gain, shift_weight, qkv_weight, query_gain, key_gain, self_out_weight, cross_norm_gain, cross_query_weight, text_kv_weight, cross_query_gain, cross_key_gain, cross_out_weight, ffn_norm_gain, ffn_up_weight, ffn_down_weight):
    groups, length = (hidden.shape[0], hidden.shape[1])
    joined = jnp.concatenate([hidden, skipped], axis=-1)
    normed_skip = low(layer_norm(joined, skip_gain))
    stream_one = low_back(project(normed_skip, skip_weight))
    shift_vec = project(shift_embed, shift_weight)
    normed_one = low(layer_norm(stream_one, self_norm_gain) + shift_vec[:, None, :])
    qkv_all = low_back(project(normed_one, qkv_weight)).reshape(groups, length, 3, H, HD)
    queries = low_back(low(rotate(layer_norm(qkv_all[:, :, 0], query_gain), tables)))
    keys_rot = low_back(low(rotate(layer_norm(qkv_all[:, :, 1], key_gain), tables)))
    values_in = low_back(low(qkv_all[:, :, 2]))
    heads_out = attend(jnp.swapaxes(queries, 1, 2), jnp.swapaxes(keys_rot, 1, 2), jnp.swapaxes(values_in, 1, 2))
    heads_out = low_back(low(jnp.swapaxes(heads_out, 1, 2).reshape(groups, length, D)))
    stream_two = stream_one + low_back(project(heads_out, self_out_weight))
    normed_two = low(layer_norm(stream_two, cross_norm_gain))
    cross_raw = low_back(project(normed_two, cross_query_weight)).reshape(groups, length, H, HD)
    cross_queries = low_back(low(layer_norm(cross_raw, cross_query_gain)))
    text_kv = low_back(jnp.einsum('gmc,che->gmhe', text_rows, text_kv_weight, precision=highest, preferred_element_type=jnp.float32))
    text_keys = low(layer_norm(text_kv[..., :HD], cross_key_gain))
    text_values = low(text_kv[..., HD:])
    cross_out = attend(jnp.swapaxes(cross_queries, 1, 2), jnp.swapaxes(text_keys, 1, 2), jnp.swapaxes(text_values, 1, 2))
    cross_out = low_back(low(jnp.swapaxes(cross_out, 1, 2).reshape(groups, length, D)))
    stream_three = stream_two + low_back(project(cross_out, cross_out_weight))
    normed_three = low(layer_norm(stream_three, ffn_norm_gain))
    ffn_hidden = low_back(project(normed_three, ffn_up_weight))
    activated = low(jax.nn.gelu(ffn_hidden, approximate=True))
    return stream_three + low_back(project(activated, ffn_down_weight))

def reference(hidden_in, skip_in, text_states, timesteps, positions, cotangent, skip_gain, skip_weight, self_norm_gain, shift_weight, qkv_weight, query_gain, key_gain, self_out_weight, cross_norm_gain, cross_query_weight, text_kv_weight, cross_query_gain, cross_key_gain, cross_out_weight, ffn_norm_gain, ffn_up_weight, ffn_down_weight):
    params = (skip_gain.astype(jnp.float32), skip_weight.astype(jnp.float32), self_norm_gain.astype(jnp.float32), shift_weight.astype(jnp.float32), qkv_weight.astype(jnp.float32), query_gain.astype(jnp.float32), key_gain.astype(jnp.float32), self_out_weight.astype(jnp.float32), cross_norm_gain.astype(jnp.float32), cross_query_weight.astype(jnp.float32), text_kv_weight.astype(jnp.float32), cross_query_gain.astype(jnp.float32), cross_key_gain.astype(jnp.float32), cross_out_weight.astype(jnp.float32), ffn_norm_gain.astype(jnp.float32), ffn_up_weight.astype(jnp.float32), ffn_down_weight.astype(jnp.float32))
    shift_embed = low(jax.nn.silu(time_embed(timesteps, D)))
    tables = rope_tables(positions, HD)
    group_size = math.gcd(LATENTS, max(1, 4096 // L))
    group_count = LATENTS // group_size

    def regroup(array):
        return array.reshape((group_count, group_size) + array.shape[1:])
    stacked = (regroup(hidden_in), regroup(skip_in), regroup(text_states), regroup(shift_embed), tuple((regroup(table) for table in tables)), regroup(cotangent))

    def step_group(totals, inputs):
        hidden_part, skip_part, text_part, embed_part, table_part, cot_part = inputs

        def layer_of(hidden, skipped, text_rows, *weights):
            return layer_forward(hidden, skipped, text_rows, embed_part, table_part, *weights)
        output, pullback = jax.vjp(layer_of, hidden_part.astype(jnp.float32), skip_part.astype(jnp.float32), text_part.astype(jnp.float32), *params)
        gradients = pullback(cot_part.astype(jnp.float32))
        totals = tuple((running + fresh for running, fresh in zip(totals, gradients[3:])))
        return (totals, (output.astype(jnp.bfloat16), gradients[0].astype(jnp.bfloat16), gradients[1].astype(jnp.bfloat16), gradients[2].astype(jnp.bfloat16)))
    zero_init = tuple((jnp.zeros(weight.shape, jnp.float32) for weight in params))
    totals, results = lax.scan(step_group, zero_init, stacked)

    def flatten(array):
        return array.reshape((LATENTS,) + array.shape[2:])
    return (flatten(results[0]), flatten(results[1]), flatten(results[2]), flatten(results[3]), totals[0], totals[1], totals[2], totals[3], totals[4], totals[5], totals[6], totals[7], totals[8], totals[9], totals[10], totals[11], totals[12], totals[13], totals[14], totals[15], totals[16])
```

```python
import math

import jax
import jax.numpy as jnp
from jax import lax
from jax.experimental import pallas as pl
from jax.experimental.pallas import tpu as pltpu
from jax.sharding import Mesh, PartitionSpec as P

H = 16
HD = 88
SCALE = HD ** (-0.5)
norm_eps = 1e-06
F32 = jnp.float32
BF = jnp.bfloat16
SEQ = ("z", "x")
SMALL = pl.CostEstimate(flops=1024, bytes_accessed=1024, transcendentals=0)


def dot(left, right, left_dim, right_dim):
    return lax.dot_general(
        left, right, (((left_dim,), (right_dim,)), ((), ())), preferred_element_type=F32
    )


def norm_stats(tensor, axis):
    mean = jnp.mean(tensor, axis=axis, keepdims=True)
    center = tensor - mean
    spread = jnp.mean(center * center, axis=axis, keepdims=True)
    return mean, lax.rsqrt(spread + norm_eps)


def norm_back(grad, tensor, mean, rstd, gain, axis):
    normed = (tensor - mean) * rstd
    scaled = grad * gain
    first = jnp.mean(scaled, axis=axis, keepdims=True)
    second = jnp.mean(scaled * normed, axis=axis, keepdims=True)
    return rstd * (scaled - first - normed * second), grad * normed


def time_embed(step_ids, embed_width):
    half_width = embed_width // 2
    frequency = jnp.exp(-math.log(10000.0) * jnp.arange(half_width, dtype=F32) / half_width)
    angles = step_ids.astype(F32)[:, None] * frequency[None, :]
    return jnp.concatenate([jnp.cos(angles), jnp.sin(angles)], axis=-1)


def rope_tables(grid_pos):
    quarter = HD // 4
    frequency = jnp.exp(-math.log(10000.0) * jnp.arange(quarter, dtype=F32) / quarter)
    row = frequency[:, None] * grid_pos[:, 0, :].astype(F32).reshape(1, -1)
    col = frequency[:, None] * grid_pos[:, 1, :].astype(F32).reshape(1, -1)
    nil = jnp.zeros_like(row)
    cos_row, sin_row, cos_col, sin_col = jnp.cos(row), jnp.sin(row), jnp.cos(col), jnp.sin(col)
    own = jnp.concatenate([cos_row, cos_row, cos_col, cos_col], axis=0)
    upper = jnp.concatenate([-sin_row, nil, -sin_col, nil], axis=0)
    lower = jnp.concatenate([nil, sin_row, nil, sin_col], axis=0)
    return own, upper, lower


def qkv_norm_kernel(raw_ref, gain_ref, own_ref, upper_ref, lower_ref, out_ref):
    quarter = HD // 4
    for i in range(raw_ref.shape[1]):
        for kind in range(2):
            raw = raw_ref[kind, i]
            mean, rstd = norm_stats(raw, 0)
            value = (raw - mean) * rstd * gain_ref[kind]
            value = (
                value * own_ref[...]
                + pltpu.roll(value, HD - quarter, 0) * upper_ref[...]
                + pltpu.roll(value, quarter, 0) * lower_ref[...]
            )
            out_ref[0, i, kind] = value.astype(BF)
        out_ref[0, i, 2] = raw_ref[2, i].astype(BF)


def qkv_norm_back_kernel(
    grad_ref, raw_ref, gain_ref, own_ref, upper_ref, lower_ref, out_ref, sum_ref
):
    quarter = HD // 4

    @pl.when(pl.program_id(0) == 0)
    def _():
        sum_ref[...] = jnp.zeros_like(sum_ref)

    for i in range(raw_ref.shape[1]):
        for kind in range(2):
            grad = grad_ref[0, i, kind].astype(F32)
            grad = (
                grad * own_ref[...]
                + pltpu.roll(grad * upper_ref[...], quarter, 0)
                + pltpu.roll(grad * lower_ref[...], HD - quarter, 0)
            )
            raw = raw_ref[kind, i]
            mean, rstd = norm_stats(raw, 0)
            back, part = norm_back(grad, raw, mean, rstd, gain_ref[kind], 0)
            out_ref[kind, i] = back.astype(BF)
            sum_ref[kind] += jnp.sum(part, axis=1, keepdims=True)
        out_ref[2, i] = grad_ref[0, i, 2]


def qkv_norm_call(grads, raw, gains, tables, groups, name):
    kinds, heads, features, tokens = raw.shape
    own = heads // groups
    by_kind = pl.BlockSpec((kinds, own, features, tokens), lambda i: (0, i, 0, 0))
    by_group = pl.BlockSpec((1, own, kinds, features, tokens), lambda i: (i, 0, 0, 0, 0))
    table = pl.BlockSpec((features, tokens), lambda i: (0, 0))
    column = pl.BlockSpec((2, features, 1), lambda i: (0, 0, 0))
    group_shape = jax.ShapeDtypeStruct((groups, own, kinds, features, tokens), BF)
    kind_shape = jax.ShapeDtypeStruct(raw.shape, BF)
    total = jax.ShapeDtypeStruct((2, features, 1), F32)
    back = grads is not None
    return pl.pallas_call(
        qkv_norm_back_kernel if back else qkv_norm_kernel,
        grid=(groups,),
        in_specs=([by_group] if back else []) + [by_kind, column] + [table] * 3,
        out_specs=[by_kind, column] if back else by_group,
        out_shape=[kind_shape, total] if back else group_shape,
        compiler_params=pltpu.CompilerParams(vmem_limit_bytes=32 * 2**20),
        cost_estimate=SMALL,
        name=name,
    )(*([grads] if back else []), raw, gains, *tables)


def gate(value):
    corner = value[(0,) * value.ndim].astype(F32)
    return jnp.where(corner != corner, 1.0, 0.0)


def pin_of(*values):
    return jnp.zeros((8, 128), F32) + sum(gate(value) for value in values)


def assemble_kernel(count, moves, starts, *refs):
    pieces, out, sems = refs[:count], refs[count], refs[count + 1]
    copies = [
        pltpu.make_async_copy(
            pieces[piece].at[pl.ds(source, size)],
            out.at[pl.ds(pl.multiple_of(starts[i], 16), size)],
            sems.at[i],
        )
        for i, (piece, source, size) in enumerate(moves)
    ]
    for copy in copies:
        copy.start()
    for copy in copies:
        copy.wait()


def assemble(pieces, moves, starts, rows):
    columns, dtype = pieces[0].shape[1], pieces[0].dtype
    if columns % 128 or any(source % 16 or size % 16 for _, source, size in moves):
        full = jnp.zeros((rows, columns), dtype)
        for (piece, source, size), start in zip(moves, starts):
            block = pieces[piece][source : source + size]
            full = lax.dynamic_update_slice_in_dim(full, block, start, axis=0)
        return full
    count = len(pieces)
    anywhere = pl.BlockSpec(memory_space=pl.ANY)

    def kernel(starts_ref, *refs):
        assemble_kernel(count, moves, starts_ref, *refs)

    return pl.pallas_call(
        kernel,
        out_shape=jax.ShapeDtypeStruct((rows, columns), dtype),
        grid_spec=pltpu.PrefetchScalarGridSpec(
            num_scalar_prefetch=1,
            grid=(1,),
            in_specs=[anywhere] * count,
            out_specs=pl.BlockSpec(memory_space=pltpu.VMEM),
            scratch_shapes=[pltpu.SemaphoreType.DMA((len(moves),))],
        ),
        compiler_params=pltpu.CompilerParams(vmem_limit_bytes=32 * 2**20),
        cost_estimate=SMALL,
        name="assemble",
    )(jnp.stack([jnp.asarray(start, jnp.int32) for start in starts]), *pieces)


def wide(ref, kind, first, count):
    return jnp.concatenate([ref[first + i, 0, kind] for i in range(count)], axis=1)


def contract(left, right, left_dim, right_dim):
    return lax.dot_general(
        left, right, (((left_dim,), (right_dim,)), ((), ())), preferred_element_type=F32
    )


def attend_forward_kernel(step, qkv_ref, pin_ref, out_ref, log_ref):
    blocks, lanes = qkv_ref.shape[0], qkv_ref.shape[4]
    k, v = wide(qkv_ref, 1, 0, blocks), wide(qkv_ref, 2, 0, blocks)
    for first in range(0, blocks, step):
        q = wide(qkv_ref, 0, first, step)
        scores = SCALE * contract(k, q, 0, 0)
        top = jnp.max(scores, axis=0, keepdims=True)
        weights = jnp.exp(scores - top)
        total = jnp.sum(weights, axis=0, keepdims=True)
        out = contract(v, weights.astype(BF), 1, 0) / total
        log_ref[0, 0, :, first * lanes : (first + step) * lanes] = top + jnp.log(total)
        for i in range(step):
            out_ref[first + i, 0, 0] = out[:, i * lanes : (i + 1) * lanes].astype(BF)


def attend_backward_kernel(step, qkv_ref, log_ref, g_ref, pin_ref, out_ref):
    blocks, lanes = qkv_ref.shape[0], qkv_ref.shape[4]
    k, v = wide(qkv_ref, 1, 0, blocks), wide(qkv_ref, 2, 0, blocks)
    dk = jnp.zeros((k.shape[0], k.shape[1]), F32)
    dv = dk
    for first in range(0, blocks, step):
        q, g = wide(qkv_ref, 0, first, step), wide(g_ref, 0, first, step)
        log_sum = log_ref[0, 0, :, first * lanes : (first + step) * lanes]
        probs = jnp.exp(SCALE * contract(k, q, 0, 0) - log_sum)
        grad_probs = contract(v, g, 0, 0)
        delta = jnp.sum(grad_probs * probs, axis=0, keepdims=True)
        grad_scores = (probs * (grad_probs - delta)).astype(BF)
        dq = SCALE * contract(k, grad_scores, 1, 0)
        dk = dk + contract(q, grad_scores, 1, 1)
        dv = dv + contract(g, probs.astype(BF), 1, 1)
        for i in range(step):
            out_ref[first + i, 0, 0] = dq[:, i * lanes : (i + 1) * lanes].astype(BF)
    for i in range(blocks):
        out_ref[i, 0, 1] = (SCALE * dk[:, i * lanes : (i + 1) * lanes]).astype(BF)
        out_ref[i, 0, 2] = dv[:, i * lanes : (i + 1) * lanes].astype(BF)


def attention_call(kernel, arrays, batch, made, name, pin):
    blocks, heads, _, _, lanes = arrays[0].shape
    lanes //= batch

    def spec(kinds):
        if kinds:
            return pl.BlockSpec((blocks, 1, kinds, HD, lanes), lambda b, h: (0, h, 0, 0, b))
        return pl.BlockSpec((1, 1, 1, blocks * lanes), lambda b, h: (b, h, 0, 0))

    def shape(kinds):
        if kinds:
            return jax.ShapeDtypeStruct((blocks, heads, kinds, HD, batch * lanes), BF)
        return jax.ShapeDtypeStruct((batch, heads, 1, blocks * lanes), F32)

    step = max(1, min(blocks, 256 // lanes))
    body = lambda *refs: kernel(step, *refs)
    return pl.pallas_call(
        body,
        grid=(batch, heads),
        in_specs=[spec(a.shape[2] if a.ndim == 5 else 0) for a in arrays]
        + [pl.BlockSpec((8, 128), lambda b, h: (0, 0))],
        out_specs=[spec(kinds) for kinds in made],
        out_shape=[shape(kinds) for kinds in made],
        compiler_params=pltpu.CompilerParams(vmem_limit_bytes=48 * 2**20),
        cost_estimate=SMALL,
        name=name,
    )(*arrays, pin)


def local(
    hidden_in,
    skip_in,
    text_states,
    timesteps,
    positions,
    cotangent,
    skip_gain,
    skip_weight,
    self_norm_gain,
    shift_weight,
    qkv_weight,
    query_gain,
    key_gain,
    self_out_weight,
    cross_norm_gain,
    cross_query_weight,
    text_kv_weight,
    cross_query_gain,
    cross_key_gain,
    cross_out_weight,
    ffn_norm_gain,
    ffn_up_weight,
    ffn_down_weight,
):
    n_dp, n_seq = lax.axis_size("dp"), lax.axis_size(SEQ)
    me_dp, me_x = lax.axis_index("dp"), lax.axis_index("x")
    batch, length, width = hidden_in.shape
    rows = batch * length
    group_heads = H // n_seq
    text_len = text_states.shape[1]


    def dperm(value, mask):
        return lax.ppermute(value, "dp", [(i, i ^ mask) for i in range(n_dp)])

    def xperm(value):
        return lax.ppermute(value, "x", [(0, 1), (1, 0)])

    def zperm(value, mask):
        return lax.ppermute(value, "z", [(i, i ^ mask) for i in range(n_seq // 2)])

    def mixed(value, first, second):
        sizes = {"dp": n_dp, "z": n_seq // 2, "x": 2}

        def number(place):
            return (place["dp"] * sizes["z"] + place["z"]) * 2 + place["x"]

        pairs = []
        for d in range(n_dp):
            for z in range(sizes["z"]):
                for x in range(2):
                    place = {"dp": d, "z": z, "x": x}
                    axis, mask = second if d & 1 else first
                    pairs.append((number(place), number({**place, axis: place[axis] ^ mask})))
        return lax.ppermute(value, ("dp", "z", "x"), pairs)

    core, far_bit = me_dp & 1, (me_dp >> 1) & 1
    z_bit = lax.axis_index("z") & 1
    in_z, in_x, in_far = ("z", 1), ("x", 1), ("dp", 2)

    def by_core(first, second):
        return jnp.where(core == 1, second, first)

    def rows_at(value, start, count):
        return lax.dynamic_slice_in_dim(value, start, count, axis=0)

    def at(value, place):
        return lax.dynamic_index_in_dim(value, place, 0, keepdims=False)

    far_masks = list(range(2, n_dp, 2))

    def held(value, token):
        return (value.astype(F32) + gate(token)).astype(value.dtype)

    def gather_weights(shards, token=None, start=None):
        number, (count, columns) = len(shards), shards[0].shape
        half = count // 2
        shard = jnp.concatenate(shards, axis=0) if number > 1 else shards[0]
        if start is not None:
            shard = held(shard, start)
        pieces, places = [shard, dperm(shard, 1)], [(me_dp, None), (me_dp ^ 1, None)]
        if token is None:
            halves = shard.reshape(number, 2, half, columns)
            mine = by_core(me_x, z_bit)
            part = lax.dynamic_index_in_dim(halves, mine, 1, keepdims=False).reshape(-1, columns)
        for mask in far_masks:
            far, both = me_dp ^ mask, me_dp ^ mask ^ 1
            if token is None:
                near = dperm(part, mask)
                other = mixed(near, in_x, in_z)
                pieces += [near, other, dperm(near, 1), dperm(other, 1)]
                theirs = by_core(z_bit, me_x)
                places += [(far, mine), (far, 1 - mine), (both, theirs), (both, 1 - theirs)]
            else:
                near = held(dperm(shard, mask), token)
                pieces += [near, dperm(near, 1)]
                places += [(far, None), (both, None)]
        gathered, arrived = [], pieces[2]
        for i in range(number):
            moves, starts = [], []
            for j, (owner, which) in enumerate(places):
                size = count if which is None else half
                moves.append((j, i * size, size))
                starts.append(owner * count + (0 if which is None else which * half))
            gathered.append(assemble(pieces, moves, starts, n_dp * count))
        return gathered, arrived

    def split_masks():
        masks, mask = [], n_dp // 2
        while mask:
            masks.append(mask)
            mask //= 2
        return masks

    dp_masks = split_masks()

    def gather_tokens(value, token=None):
        for mask in dp_masks:
            got = dperm(value, mask)
            if token is not None and mask != 1:
                got = held(got, token)
            value = jnp.concatenate([value, got], axis=0)
        return value

    def scatter_tokens(value):
        for mask in reversed(dp_masks):
            half = value.shape[0] // 2
            value = value[:half] + dperm(value[half:].astype(BF), mask).astype(F32)
        return value

    def plus(left, right, *tokens):
        total = left.astype(F32) + right.astype(F32)
        for token in tokens:
            if token is not None:
                total = total + gate(token)
        return total.astype(BF)

    def joined_pair(part, other, axis):
        upper = me_x == 1
        pair = [jnp.where(upper, other, part), jnp.where(upper, part, other)]
        return jnp.concatenate(pair, axis=axis)

    def split_pair(value, axis, which):
        return (
            lax.dynamic_index_in_dim(value, which, axis, keepdims=False),
            lax.dynamic_index_in_dim(value, 1 - which, axis, keepdims=False),
        )

    def quarter_pair(own, token=None):
        pair = jnp.stack([own, mixed(own, in_z, in_x)])
        return pair if token is None else held(pair, token)

    def quarters_in_order(pair, axis):
        stack = jnp.concatenate([pair, mixed(pair, in_x, in_z)], axis=0)
        pieces = []
        for x in range(2):
            for z in range(2):
                rx, rz = me_x ^ x, z_bit ^ z
                pieces.append(at(stack, by_core(2 * rx + rz, 2 * rz + rx)))
        return jnp.concatenate(pieces, axis=axis).astype(F32)

    def far_along_z(value, token):
        mask = 2
        while mask < n_seq // 2:
            value = plus(value, zperm(value, mask), token)
            mask *= 2
        return value

    def shard_sums(blocks):
        number, (_, _, count, columns) = len(blocks), blocks[0].shape

        def side(which):
            size = (n_dp // 2, 1, count, columns)
            picked = [lax.dynamic_slice(b, (0, which, 0, 0), size) for b in blocks]
            return jnp.concatenate(picked, axis=1)

        mine, got = side(core), dperm(side(1 - core), 1)
        token = yield got
        size, mask, bits = n_dp // 2, n_dp // 4, me_dp >> 1
        while size > 2:
            mine, got = plus(mine, got, token), None
            here = bits & mask
            mine = mine.reshape((2, size // 2) + mine.shape[1:])
            keep, send = split_pair(mine, 0, jnp.where(here != 0, 1, 0))
            mine, got = keep, dperm(send, 2 * mask)
            size, mask = size // 2, mask // 2

        def block(which, first, second):
            far = far_bit ^ by_core(first, second)
            x = me_x ^ by_core(second, first)
            begin = (far, 0, x * (count // 2), 0)
            size = (1, number, count // 2, columns)
            return lax.dynamic_slice(which, begin, size)[0]

        def total(first, second):
            return plus(block(mine, first, second), block(got, first, second), token)

        sent = jnp.stack([total(1, 0), total(1, 1)])
        held_back = [total(0, 0), total(0, 1)]
        token = yield sent
        got = mixed(sent, in_far, in_x)
        send = plus(held_back[1], got[1], token)
        own = plus(held_back[0], got[0], token)
        token = yield send
        own = plus(own, mixed(send, in_x, in_far), token)
        size = (number, count // 4, columns)
        keep = lax.dynamic_slice(own, (0, z_bit * (count // 4), 0), size)
        send = lax.dynamic_slice(own, (0, (1 - z_bit) * (count // 4), 0), size)
        token = yield send
        own = plus(keep, zperm(send, 1), token)
        token = yield own
        own = far_along_z(own, token)
        token = yield own
        if token is not None:
            own = held(own, token)
        full = quarters_in_order(quarter_pair(own), 1)
        yield [full[i] for i in range(number)]

    def as_shards(grad):
        return grad.reshape((n_dp // 2, 2, -1) + grad.shape[1:])

    def sum_all(vector):
        for mask in dp_masks:
            vector = vector + dperm(vector, mask)
        vector = vector + xperm(vector)
        mask = 1
        while mask < n_seq // 2:
            vector = vector + zperm(vector, mask)
            mask *= 2
        return vector


    (skip_full,), _ = gather_weights([skip_weight])
    (qkv_full,), _ = gather_weights([qkv_weight])
    text_weight = text_kv_weight.reshape(text_kv_weight.shape[0], -1)
    text_count = text_weight.shape[0]
    text_pieces, text_marks = [text_weight], [0]
    for mask in dp_masks:
        text_pieces = text_pieces + [dperm(piece, mask) for piece in text_pieces]
        text_marks = text_marks + [mark ^ mask for mark in text_marks]
    text_weight = assemble(
        text_pieces,
        [(i, 0, text_count) for i in range(n_dp)],
        [(me_dp ^ mark) * text_count for mark in text_marks],
        n_dp * text_count,
    )
    text_weight = text_weight.reshape((-1,) + text_kv_weight.shape[1:])

    hidden_part = ffn_up_weight.shape[1] // n_dp
    up_rows = ffn_up_weight.shape[0]
    up_blocks = jnp.stack(
        [ffn_up_weight[:, i * hidden_part : (i + 1) * hidden_part] for i in range(n_dp)]
    )
    cot_rows = cotangent.reshape(rows, width)

    def gather_up(token):
        pieces = []
        for mask in range(n_dp):
            block = at(up_blocks, me_dp ^ mask)
            if mask:
                block = dperm(block, mask)
            pieces.append(held(block, token) if mask > 1 else block)
        return pieces[2:], assemble(
            pieces,
            [(i, 0, up_rows) for i in range(n_dp)],
            [(me_dp ^ mask) * up_rows for mask in range(n_dp)],
            n_dp * up_rows,
        )


    text_full = lax.all_gather(text_states, SEQ, axis=2, tiled=True)
    text_kv = jnp.einsum("che,bmc->bhem", text_weight, text_full, preferred_element_type=F32)
    tk_raw = text_kv[:, :, :HD]
    tk_mean, tk_rstd = norm_stats(tk_raw, -2)
    ck_gain = cross_key_gain[:, None]
    tkv_own = jnp.concatenate(
        [((tk_raw - tk_mean) * tk_rstd * ck_gain).astype(BF), text_kv[:, :, HD:].astype(BF)], axis=2
    )
    tkv_all = lax.all_gather(tkv_own, SEQ, axis=1, tiled=True)
    tk_all, tv_all = tkv_all[:, :, :HD], tkv_all[:, :, HD:]


    shift_rows = shift_weight.shape[0]
    all_steps = lax.dynamic_update_slice_in_dim(
        jnp.zeros((n_dp * batch,), F32), timesteps.astype(F32), me_dp * batch, axis=0
    )
    for mask in dp_masks:
        all_steps = all_steps + dperm(all_steps, mask)
    embed_all = jax.nn.silu(time_embed(all_steps, width)).astype(BF)
    embed_part = lax.dynamic_slice_in_dim(embed_all, me_dp * shift_rows, shift_rows, axis=1)
    shift_all = dot(embed_part, shift_weight, 1, 0)

    tables = rope_tables(positions)
    joined = jnp.concatenate([hidden_in, skip_in], axis=-1).reshape(rows, 2 * width).astype(F32)
    skip_mean, skip_rstd = norm_stats(joined, -1)
    skip_bf = ((joined - skip_mean) * skip_rstd * skip_gain).astype(BF)
    x1 = dot(skip_bf, skip_full, 1, 0) + gate(tkv_own)
    one_mean, one_rstd = norm_stats(x1, -1)
    for mask in reversed(dp_masks):
        shift_all = shift_all + dperm(shift_all, mask) + gate(x1)
    shift_vec = rows_at(shift_all, me_dp * batch, batch)
    shift_tokens = jnp.repeat(shift_vec, length, axis=0)
    first_bf = ((x1 - one_mean) * one_rstd * self_norm_gain + shift_tokens).astype(BF)
    qkv_raw = dot(qkv_full, first_bf, 0, 1).reshape(3, H, HD, rows)
    qk_gain = jnp.stack([query_gain, key_gain])[:, :, None]
    direct = length % 128 == 0

    def exchange(value):
        return lax.all_to_all(value, SEQ, split_axis=0, concat_axis=0, tiled=True)

    def to_heads(value):
        kinds = value.shape[2]
        value = exchange(value)
        if not direct:
            value = value.reshape(n_seq, group_heads, kinds, HD, batch, length)
            value = value.transpose(1, 2, 3, 4, 0, 5)
            value = value.reshape(1, group_heads, kinds, HD, batch * n_seq * length)
        return value

    def to_tokens(value):
        kinds = value.shape[2]
        if not direct:
            value = value.reshape(group_heads, kinds, HD, batch, n_seq, length)
            value = value.transpose(4, 0, 1, 2, 3, 5)
            value = value.reshape(n_seq, group_heads, kinds, HD, rows)
        return exchange(value)

    qkv = to_heads(qkv_norm_call(None, qkv_raw, qk_gain, tables, n_seq, "qkv_norm"))
    (self_out_full, cross_query_full, cross_out_full), out_arrived = gather_weights(
        [self_out_weight, cross_query_weight, cross_out_weight], qkv, x1
    )
    out, log_sum = attention_call(
        attend_forward_kernel, [qkv], batch, [1, 0], "attend_forward", pin_of(out_arrived)
    )
    self_tokens = to_tokens(out).reshape(width, rows)
    up_arrived, up_part = gather_up(out)
    cot_all = gather_tokens(cot_rows, self_tokens)
    x2 = x1 + dot(self_tokens, self_out_full, 0, 0) + sum(gate(p) for p in up_arrived)
    two_mean, two_rstd = norm_stats(x2, -1)
    second_bf = ((x2 - two_mean) * two_rstd * cross_norm_gain).astype(BF)

    cq_raw = dot(cross_query_full, second_bf, 0, 1).reshape(H, HD, rows)
    cq_mean, cq_rstd = norm_stats(cq_raw, -2)
    cq_gain = cross_query_gain[:, None]
    cq = ((cq_raw - cq_mean) * cq_rstd * cq_gain).astype(BF).reshape(H, HD, batch, length)
    cross_scores = SCALE * jnp.einsum("hebq,bhem->bhqm", cq, tk_all, preferred_element_type=F32)
    cross_max = jnp.max(cross_scores, axis=-1, keepdims=True)
    cross_exp = jnp.exp(cross_scores - cross_max)
    cross_probs = cross_exp / jnp.sum(cross_exp, axis=-1, keepdims=True)
    cross_probs_bf = cross_probs.astype(BF)
    cross_tokens = (
        jnp.einsum("bhqm,bhem->hebq", cross_probs_bf, tv_all, preferred_element_type=F32)
        .astype(BF)
        .reshape(width, rows)
    )
    x3 = x2 + dot(cross_tokens, cross_out_full, 0, 0)
    three_mean, three_rstd = norm_stats(x3, -1)
    third_bf = ((x3 - three_mean) * three_rstd * ffn_norm_gain).astype(BF)

    third_all = gather_tokens(third_bf)
    up = dot(up_part, third_all, 0, 1)
    active, gelu_pull = jax.vjp(lambda value: jax.nn.gelu(value, approximate=True), up)
    active_bf = active.astype(BF)
    grad_active = dot(ffn_down_weight, cot_all, 1, 1)
    grad_up = gelu_pull(grad_active)[0].astype(BF)
    grad_three_norm = scatter_tokens(dot(grad_up, up_part, 0, 1))
    block_out = x3 + scatter_tokens(dot(active_bf, ffn_down_weight, 0, 0))


    sub = hidden_part // 4

    def hidden_rows(value, first):
        pieces = []
        for second in range(2):
            x, z = me_x ^ by_core(first, second), z_bit ^ by_core(second, first)
            pieces.append(rows_at(value, (2 * x + z) * sub, sub))
        return jnp.concatenate(pieces, axis=0)

    def hidden_sums(left, right):
        sent = dot(hidden_rows(left, 1), right, 1, 0).astype(BF)
        kept = dot(hidden_rows(left, 0), right, 1, 0).astype(BF)
        token = yield sent
        got = mixed(sent, in_x, in_z)
        send = plus(kept[sub:], got[sub:], token)
        own = plus(kept[:sub], got[:sub], token)
        token = yield send
        own = plus(own, mixed(send, in_z, in_x), token)
        token = yield own
        own = far_along_z(own, token)
        token = yield own
        yield own if token is None else held(own, token)

    down = hidden_sums(active_bf, cot_all)
    up_back = hidden_sums(grad_up, third_all)
    first_sent = [next(down), next(up_back)]

    def up_pair(part, token):
        blocks = part.T.reshape(n_dp, up_rows, sub)
        own = [at(blocks, me_dp)] + [dperm(at(blocks, me_dp ^ m), m) for m in range(1, n_dp)]
        own = jnp.stack(own)
        return quarter_pair(jnp.stack([at(own, me_dp ^ i) for i in range(n_dp)]), token)


    grad_three_norm = grad_three_norm + (
        gate(first_sent[0]) + gate(first_sent[1]) + gate(up_back.send(None))
    )
    back_three, ffn_gain_rows = norm_back(
        grad_three_norm, x3, three_mean, three_rstd, ffn_norm_gain, -1
    )
    grad_three = cot_rows.astype(F32) + back_three
    grad_three_bf = grad_three.astype(BF)
    grad_cross = dot(cross_out_full, grad_three_bf, 1, 1).astype(BF).reshape(H, HD, batch, length)
    grad_cprobs = jnp.einsum("hebq,bhem->bhqm", grad_cross, tv_all, preferred_element_type=F32)
    cross_dot = jnp.sum(grad_cprobs * cross_probs, axis=-1, keepdims=True)
    grad_cscores = (cross_probs * (grad_cprobs - cross_dot)).astype(BF)
    grad_cq = (
        SCALE * jnp.einsum("bhqm,bhem->hebq", grad_cscores, tk_all, preferred_element_type=F32)
    ).astype(BF)
    grad_tk = SCALE * jnp.einsum("bhqm,hebq->hbem", grad_cscores, cq, preferred_element_type=F32)
    grad_tv = jnp.einsum("bhqm,hebq->hbem", cross_probs_bf, grad_cross, preferred_element_type=F32)
    grad_tkv = jnp.concatenate([grad_tk, grad_tv], axis=2).astype(BF)
    grad_tkv = grad_tkv.reshape((n_seq // 2, 2, group_heads) + grad_tkv.shape[1:])
    tkv_keep, tkv_send = split_pair(grad_tkv, 1, me_x)
    tkv_got = xperm(tkv_send)

    sent = gate(up_back.send(grad_three_bf)) + gate(down.send(grad_three_bf))
    back_cq, cq_gain_rows = norm_back(
        grad_cq.reshape(H, HD, rows).astype(F32), cq_raw, cq_mean, cq_rstd, cq_gain + sent, -2
    )
    grad_cq_raw = back_cq.astype(BF).reshape(width, rows)
    grad_two_norm = dot(grad_cq_raw, cross_query_full, 0, 1)
    sent = gate(down.send(grad_cq_raw))
    back_two, cross_gain_rows = norm_back(
        grad_two_norm, x2, two_mean, two_rstd, cross_norm_gain + sent, -1
    )
    grad_two = grad_three + back_two
    grad_two_bf = grad_two.astype(BF)
    middle = shard_sums(
        [
            as_shards(dot(cross_tokens, grad_three_bf, 1, 0).astype(BF)),
            as_shards(dot(second_bf, grad_cq_raw, 0, 1).astype(BF)),
            as_shards(dot(self_tokens, grad_two_bf, 1, 0).astype(BF)),
        ]
    )
    next(middle)
    grad_out = dot(self_out_full, grad_two_bf, 1, 1).astype(BF)
    grad_out = to_heads(grad_out.reshape(n_seq, group_heads, 1, HD, rows))
    pin = pin_of(middle.send(grad_two_bf))
    (grad_heads,) = attention_call(
        attend_backward_kernel, [qkv, log_sum, grad_out], batch, [3], "attend_backward", pin
    )
    grad_tokens = to_tokens(grad_heads)
    middle_x = middle.send(grad_heads)
    back_qkv, qk_gain_sum = qkv_norm_call(
        grad_tokens, qkv_raw, qk_gain + gate(middle_x), tables, n_seq, "qkv_norm_back"
    )
    back_qkv = back_qkv.reshape(3 * width, rows)
    late = shard_sums([as_shards(dot(first_bf, back_qkv, 0, 1).astype(BF))])
    next(late)
    grad_one_norm = dot(back_qkv, qkv_full, 0, 1)
    middle_z = middle.send(back_qkv)
    late_far = late.send(back_qkv)
    grad_one_norm = grad_one_norm + (gate(middle_z) + gate(late_far))
    shift_part = jnp.sum(grad_one_norm.reshape(batch, length, width), axis=1)
    back_one, self_gain_rows = norm_back(
        grad_one_norm, x1, one_mean, one_rstd, self_norm_gain, -1
    )
    grad_one_bf = (grad_two + back_one).astype(BF)
    skip_blocks = dot(skip_bf, grad_one_bf, 0, 0).astype(BF)
    skip_blocks = skip_blocks.reshape(n_dp // 2, 2, 2, -1, width)
    end = shard_sums([skip_blocks[:, :, i] for i in range(2)])
    next(end)
    grad_skip_norm = dot(grad_one_bf, skip_full, 1, 1)
    grad_tkv = plus(tkv_keep, tkv_got, grad_one_bf)
    grad_tkv = lax.psum_scatter(grad_tkv, "z", scatter_dimension=0, tiled=True)
    middle_z = middle.send(grad_one_bf)
    end.send(None)
    late.send(grad_one_bf)
    back_joined, skip_gain_rows = norm_back(
        grad_skip_norm, joined, skip_mean, skip_rstd, skip_gain + gate(middle_z), -1
    )
    for half in (down, up_back):
        half.send(grad_one_bf)
    down_pair = quarter_pair(down.send(None))
    up_grad_pair = up_pair(up_back.send(None), None)
    down_grad = quarters_in_order(down_pair, 0)
    up_grad = quarters_in_order(up_grad_pair, 2).transpose(1, 0, 2).reshape(up_rows, -1)
    middle.send(None)
    cross_out_grad, cross_query_grad, self_out_grad = middle.send(None)
    for _ in range(3):
        late.send(None)
    (qkv_grad,) = late.send(None)
    for _ in range(4):
        end.send(None)
    skip_parts = end.send(None)
    skip_grad_w = jnp.concatenate(skip_parts, axis=0)
    back_joined = back_joined.astype(BF).reshape(batch, length, 2 * width)


    grad_tkv = grad_tkv.reshape(grad_tkv.shape[1:]).astype(F32) + gate(grad_one_bf)
    grad_tkv = grad_tkv.swapaxes(0, 1)
    back_tk, ck_gain_rows = norm_back(
        grad_tkv[:, :, :HD], tk_raw, tk_mean, tk_rstd, ck_gain, -2
    )
    grad_tkv_bf = jnp.concatenate([back_tk, grad_tkv[:, :, HD:]], axis=2).astype(BF)
    text_kv_grad = jnp.einsum("bmc,bhem->che", text_full, grad_tkv_bf, preferred_element_type=F32)
    text_part = jnp.einsum("bhem,che->cbm", grad_tkv_bf, text_weight, preferred_element_type=F32)
    text_part = text_part.astype(BF).reshape(n_seq // 2, 2, -1, batch * text_len)
    text_keep, text_send = split_pair(text_part, 1, me_x)
    text_part = plus(text_keep, xperm(text_send))
    text_grad = lax.psum_scatter(text_part, "z", scatter_dimension=0, tiled=True)
    text_grad = text_grad.reshape(-1, batch, text_len).transpose(1, 2, 0)
    text_kv_grad = text_kv_grad.astype(BF).reshape(n_dp // 2, 2, text_count, -1)
    text_keep, text_send = split_pair(text_kv_grad, 1, me_dp & 1)
    text_own = plus(text_keep, dperm(text_send, 1))
    text_kv_sum = at(text_own, me_dp >> 1)
    for mask in far_masks:
        text_kv_sum = plus(text_kv_sum, dperm(at(text_own, (me_dp ^ mask) >> 1), mask))
    text_kv_sum = text_kv_sum.astype(F32).reshape(text_kv_weight.shape)


    shift_slots = lax.dynamic_update_slice_in_dim(
        jnp.zeros((n_dp * batch, width), F32), shift_part, me_dp * batch, axis=0
    )
    vectors = [
        jnp.sum(ffn_gain_rows, axis=0),
        jnp.sum(cross_gain_rows, axis=0),
        jnp.sum(self_gain_rows, axis=0),
        qk_gain_sum[0, :, 0],
        qk_gain_sum[1, :, 0],
        jnp.sum(cq_gain_rows, axis=(0, 2)),
        jnp.sum(ck_gain_rows, axis=(0, 1, 3)),
        shift_slots.reshape(-1),
    ]
    vectors.append(jnp.sum(skip_gain_rows, axis=0))
    total = sum_all(jnp.concatenate(vectors))
    sums, start = [], 0
    for vector in vectors:
        sums.append(total[start : start + vector.shape[0]])
        start += vector.shape[0]
    ffn_gain, cross_gain, self_gain, q_gain_all, k_gain_all, cq_gain_sum, ck_gain_sum = sums[:7]
    shift_total, skip_gain_sum = sums[7:]
    shift_grad = lax.dot_general(
        embed_part.astype(F32),
        shift_total.reshape(n_dp * batch, width),
        (((0,), (0,)), ((), ())),
        precision=lax.Precision.HIGHEST,
        preferred_element_type=F32,
    )

    return (
        block_out.astype(BF).reshape(batch, length, width),
        back_joined[..., :width],
        back_joined[..., width:],
        text_grad,
        skip_gain_sum,
        skip_grad_w,
        self_gain,
        shift_grad,
        qkv_grad,
        q_gain_all,
        k_gain_all,
        self_out_grad,
        cross_gain,
        cross_query_grad,
        text_kv_sum,
        cq_gain_sum,
        ck_gain_sum,
        cross_out_grad,
        ffn_gain,
        up_grad,
        down_grad,
    )


def solution(mesh):
    n_dp, n_seq = mesh.shape["dp"], mesh.shape["seq"]
    mesh = Mesh(mesh.devices.reshape(n_dp, n_seq // 2, 2), ("dp", "z", "x"))
    tokens, text, rows, none = P("dp", SEQ, None), P("dp", None, SEQ), P("dp", None), P()
    heads = P("dp", SEQ, None)
    placed = (
        tokens, tokens, text, P("dp"), text, tokens, none, rows, none, rows, rows, none, none,
        rows, none, rows, heads, none, none, rows, none, rows, rows,
    )
    given = (
        tokens, tokens, tokens, text, none, rows, none, rows, rows, none, none, rows, none, rows,
        heads, none, none, rows, none, rows, rows,
    )
    return jax.shard_map(local, mesh=mesh, in_specs=placed, out_specs=given, check_vma=False)
```

```python
import math

import jax
import jax.numpy as jnp
from jax import lax
from jax.experimental import pallas as pl
from jax.experimental.pallas import tpu as pltpu
from jax.sharding import Mesh, PartitionSpec as P

H = 16
HD = 88
SCALE = HD ** (-0.5)
norm_eps = 1e-06
F32 = jnp.float32
BF = jnp.bfloat16
SEQ = ("z", "x")
SMALL = pl.CostEstimate(flops=1024, bytes_accessed=1024, transcendentals=0)


def dot(left, right, left_dim, right_dim):
    return lax.dot_general(
        left, right, (((left_dim,), (right_dim,)), ((), ())), preferred_element_type=F32
    )


def norm_stats(tensor, axis):
    mean = jnp.mean(tensor, axis=axis, keepdims=True)
    center = tensor - mean
    spread = jnp.mean(center * center, axis=axis, keepdims=True)
    return mean, lax.rsqrt(spread + norm_eps)


def norm_back(grad, tensor, mean, rstd, gain, axis):
    normed = (tensor - mean) * rstd
    scaled = grad * gain
    first = jnp.mean(scaled, axis=axis, keepdims=True)
    second = jnp.mean(scaled * normed, axis=axis, keepdims=True)
    return rstd * (scaled - first - normed * second), grad * normed


def time_embed(step_ids, embed_width):
    half_width = embed_width // 2
    frequency = jnp.exp(-math.log(10000.0) * jnp.arange(half_width, dtype=F32) / half_width)
    angles = step_ids.astype(F32)[:, None] * frequency[None, :]
    return jnp.concatenate([jnp.cos(angles), jnp.sin(angles)], axis=-1)


def rope_tables(grid_pos):
    quarter = HD // 4
    frequency = jnp.exp(-math.log(10000.0) * jnp.arange(quarter, dtype=F32) / quarter)
    row = frequency[:, None] * grid_pos[:, 0, :].astype(F32).reshape(1, -1)
    col = frequency[:, None] * grid_pos[:, 1, :].astype(F32).reshape(1, -1)
    nil = jnp.zeros_like(row)
    cos_row, sin_row, cos_col, sin_col = jnp.cos(row), jnp.sin(row), jnp.cos(col), jnp.sin(col)
    own = jnp.concatenate([cos_row, cos_row, cos_col, cos_col], axis=0)
    upper = jnp.concatenate([-sin_row, nil, -sin_col, nil], axis=0)
    lower = jnp.concatenate([nil, sin_row, nil, sin_col], axis=0)
    return own, upper, lower


def qkv_norm_kernel(raw_ref, gain_ref, own_ref, upper_ref, lower_ref, out_ref):
    quarter = HD // 4
    for i in range(raw_ref.shape[1]):
        for kind in range(2):
            raw = raw_ref[kind, i]
            mean, rstd = norm_stats(raw, 0)
            value = (raw - mean) * rstd * gain_ref[kind]
            value = (
                value * own_ref[...]
                + pltpu.roll(value, HD - quarter, 0) * upper_ref[...]
                + pltpu.roll(value, quarter, 0) * lower_ref[...]
            )
            out_ref[0, i, kind] = value.astype(BF)
        out_ref[0, i, 2] = raw_ref[2, i].astype(BF)


def qkv_norm_back_kernel(
    grad_ref, raw_ref, gain_ref, own_ref, upper_ref, lower_ref, out_ref, sum_ref
):
    quarter = HD // 4

    @pl.when(pl.program_id(0) == 0)
    def _():
        sum_ref[...] = jnp.zeros_like(sum_ref)

    for i in range(raw_ref.shape[1]):
        for kind in range(2):
            grad = grad_ref[0, i, kind].astype(F32)
            grad = (
                grad * own_ref[...]
                + pltpu.roll(grad * upper_ref[...], quarter, 0)
                + pltpu.roll(grad * lower_ref[...], HD - quarter, 0)
            )
            raw = raw_ref[kind, i]
            mean, rstd = norm_stats(raw, 0)
            back, part = norm_back(grad, raw, mean, rstd, gain_ref[kind], 0)
            out_ref[kind, i] = back.astype(BF)
            sum_ref[kind] += jnp.sum(part, axis=1, keepdims=True)
        out_ref[2, i] = grad_ref[0, i, 2]


def qkv_norm_call(grads, raw, gains, tables, groups, name):
    kinds, heads, features, tokens = raw.shape
    own = heads // groups
    by_kind = pl.BlockSpec((kinds, own, features, tokens), lambda i: (0, i, 0, 0))
    by_group = pl.BlockSpec((1, own, kinds, features, tokens), lambda i: (i, 0, 0, 0, 0))
    table = pl.BlockSpec((features, tokens), lambda i: (0, 0))
    column = pl.BlockSpec((2, features, 1), lambda i: (0, 0, 0))
    group_shape = jax.ShapeDtypeStruct((groups, own, kinds, features, tokens), BF)
    kind_shape = jax.ShapeDtypeStruct(raw.shape, BF)
    total = jax.ShapeDtypeStruct((2, features, 1), F32)
    back = grads is not None
    return pl.pallas_call(
        qkv_norm_back_kernel if back else qkv_norm_kernel,
        grid=(groups,),
        in_specs=([by_group] if back else []) + [by_kind, column] + [table] * 3,
        out_specs=[by_kind, column] if back else by_group,
        out_shape=[kind_shape, total] if back else group_shape,
        compiler_params=pltpu.CompilerParams(vmem_limit_bytes=32 * 2**20),
        cost_estimate=SMALL,
        name=name,
    )(*([grads] if back else []), raw, gains, *tables)


def gate(value):
    corner = value[(0,) * value.ndim].astype(F32)
    return jnp.where(corner != corner, 1.0, 0.0)


def pin_of(*values):
    return jnp.zeros((8, 128), F32) + sum(gate(value) for value in values)


def assemble_kernel(count, moves, starts, *refs):
    pieces, out, sems = refs[:count], refs[count], refs[count + 1]
    copies = [
        pltpu.make_async_copy(
            pieces[piece].at[pl.ds(source, size)],
            out.at[pl.ds(pl.multiple_of(starts[i], 16), size)],
            sems.at[i],
        )
        for i, (piece, source, size) in enumerate(moves)
    ]
    for copy in copies:
        copy.start()
    for copy in copies:
        copy.wait()


def assemble(pieces, moves, starts, rows):
    columns, dtype = pieces[0].shape[1], pieces[0].dtype
    if columns % 128 or any(source % 16 or size % 16 for _, source, size in moves):
        full = jnp.zeros((rows, columns), dtype)
        for (piece, source, size), start in zip(moves, starts):
            block = pieces[piece][source : source + size]
            full = lax.dynamic_update_slice_in_dim(full, block, start, axis=0)
        return full
    count = len(pieces)
    anywhere = pl.BlockSpec(memory_space=pl.ANY)

    def kernel(starts_ref, *refs):
        assemble_kernel(count, moves, starts_ref, *refs)

    return pl.pallas_call(
        kernel,
        out_shape=jax.ShapeDtypeStruct((rows, columns), dtype),
        grid_spec=pltpu.PrefetchScalarGridSpec(
            num_scalar_prefetch=1,
            grid=(1,),
            in_specs=[anywhere] * count,
            out_specs=pl.BlockSpec(memory_space=pltpu.VMEM),
            scratch_shapes=[pltpu.SemaphoreType.DMA((len(moves),))],
        ),
        compiler_params=pltpu.CompilerParams(vmem_limit_bytes=32 * 2**20),
        cost_estimate=SMALL,
        name="assemble",
    )(jnp.stack([jnp.asarray(start, jnp.int32) for start in starts]), *pieces)


def wide(ref, kind, first, count):
    return jnp.concatenate([ref[first + i, 0, kind] for i in range(count)], axis=1)


def contract(left, right, left_dim, right_dim):
    return lax.dot_general(
        left, right, (((left_dim,), (right_dim,)), ((), ())), preferred_element_type=F32
    )


def attend_forward_kernel(step, qkv_ref, pin_ref, out_ref, log_ref):
    blocks, lanes = qkv_ref.shape[0], qkv_ref.shape[4]
    k, v = wide(qkv_ref, 1, 0, blocks), wide(qkv_ref, 2, 0, blocks)
    for first in range(0, blocks, step):
        q = wide(qkv_ref, 0, first, step)
        scores = SCALE * contract(k, q, 0, 0)
        top = jnp.max(scores, axis=0, keepdims=True)
        weights = jnp.exp(scores - top)
        total = jnp.sum(weights, axis=0, keepdims=True)
        out = contract(v, weights.astype(BF), 1, 0) / total
        log_ref[0, 0, :, first * lanes : (first + step) * lanes] = top + jnp.log(total)
        for i in range(step):
            out_ref[first + i, 0, 0] = out[:, i * lanes : (i + 1) * lanes].astype(BF)


def attend_backward_kernel(step, qkv_ref, log_ref, g_ref, pin_ref, out_ref):
    blocks, lanes = qkv_ref.shape[0], qkv_ref.shape[4]
    k, v = wide(qkv_ref, 1, 0, blocks), wide(qkv_ref, 2, 0, blocks)
    dk = jnp.zeros((k.shape[0], k.shape[1]), F32)
    dv = dk
    for first in range(0, blocks, step):
        q, g = wide(qkv_ref, 0, first, step), wide(g_ref, 0, first, step)
        log_sum = log_ref[0, 0, :, first * lanes : (first + step) * lanes]
        probs = jnp.exp(SCALE * contract(k, q, 0, 0) - log_sum)
        grad_probs = contract(v, g, 0, 0)
        delta = jnp.sum(grad_probs * probs, axis=0, keepdims=True)
        grad_scores = (probs * (grad_probs - delta)).astype(BF)
        dq = SCALE * contract(k, grad_scores, 1, 0)
        dk = dk + contract(q, grad_scores, 1, 1)
        dv = dv + contract(g, probs.astype(BF), 1, 1)
        for i in range(step):
            out_ref[first + i, 0, 0] = dq[:, i * lanes : (i + 1) * lanes].astype(BF)
    for i in range(blocks):
        out_ref[i, 0, 1] = (SCALE * dk[:, i * lanes : (i + 1) * lanes]).astype(BF)
        out_ref[i, 0, 2] = dv[:, i * lanes : (i + 1) * lanes].astype(BF)


def attention_call(kernel, arrays, batch, made, name, pin):
    blocks, heads, _, _, lanes = arrays[0].shape
    lanes //= batch

    def spec(kinds):
        if kinds:
            return pl.BlockSpec((blocks, 1, kinds, HD, lanes), lambda b, h: (0, h, 0, 0, b))
        return pl.BlockSpec((1, 1, 1, blocks * lanes), lambda b, h: (b, h, 0, 0))

    def shape(kinds):
        if kinds:
            return jax.ShapeDtypeStruct((blocks, heads, kinds, HD, batch * lanes), BF)
        return jax.ShapeDtypeStruct((batch, heads, 1, blocks * lanes), F32)

    step = max(1, min(blocks, 256 // lanes))
    body = lambda *refs: kernel(step, *refs)
    return pl.pallas_call(
        body,
        grid=(batch, heads),
        in_specs=[spec(a.shape[2] if a.ndim == 5 else 0) for a in arrays]
        + [pl.BlockSpec((8, 128), lambda b, h: (0, 0))],
        out_specs=[spec(kinds) for kinds in made],
        out_shape=[shape(kinds) for kinds in made],
        compiler_params=pltpu.CompilerParams(vmem_limit_bytes=48 * 2**20),
        cost_estimate=SMALL,
        name=name,
    )(*arrays, pin)


def local(
    hidden_in,
    skip_in,
    text_states,
    timesteps,
    positions,
    cotangent,
    skip_gain,
    skip_weight,
    self_norm_gain,
    shift_weight,
    qkv_weight,
    query_gain,
    key_gain,
    self_out_weight,
    cross_norm_gain,
    cross_query_weight,
    text_kv_weight,
    cross_query_gain,
    cross_key_gain,
    cross_out_weight,
    ffn_norm_gain,
    ffn_up_weight,
    ffn_down_weight,
):
    n_dp, n_seq = lax.axis_size("dp"), lax.axis_size(SEQ)
    me_dp, me_x = lax.axis_index("dp"), lax.axis_index("x")
    batch, length, width = hidden_in.shape
    rows = batch * length
    group_heads = H // n_seq
    text_len = text_states.shape[1]


    def dperm(value, mask):
        return lax.ppermute(value, "dp", [(i, i ^ mask) for i in range(n_dp)])

    def xperm(value):
        return lax.ppermute(value, "x", [(0, 1), (1, 0)])

    def zperm(value, mask):
        return lax.ppermute(value, "z", [(i, i ^ mask) for i in range(n_seq // 2)])

    def mixed(value, first, second):
        sizes = {"dp": n_dp, "z": n_seq // 2, "x": 2}

        def number(place):
            return (place["dp"] * sizes["z"] + place["z"]) * 2 + place["x"]

        pairs = []
        for d in range(n_dp):
            for z in range(sizes["z"]):
                for x in range(2):
                    place = {"dp": d, "z": z, "x": x}
                    axis, mask = second if d & 1 else first
                    pairs.append((number(place), number({**place, axis: place[axis] ^ mask})))
        return lax.ppermute(value, ("dp", "z", "x"), pairs)

    core, far_bit = me_dp & 1, (me_dp >> 1) & 1
    z_bit = lax.axis_index("z") & 1
    in_z, in_x, in_far = ("z", 1), ("x", 1), ("dp", 2)

    def by_core(first, second):
        return jnp.where(core == 1, second, first)

    def rows_at(value, start, count):
        return lax.dynamic_slice_in_dim(value, start, count, axis=0)

    def at(value, place):
        return lax.dynamic_index_in_dim(value, place, 0, keepdims=False)

    far_masks = list(range(2, n_dp, 2))

    def held(value, token):
        return (value.astype(F32) + gate(token)).astype(value.dtype)

    def gather_weights(shards, token=None, start=None):
        number, (count, columns) = len(shards), shards[0].shape
        half = count // 2
        shard = jnp.concatenate(shards, axis=0) if number > 1 else shards[0]
        if start is not None:
            shard = held(shard, start)
        pieces, places = [shard, dperm(shard, 1)], [(me_dp, None), (me_dp ^ 1, None)]
        if token is None:
            halves = shard.reshape(number, 2, half, columns)
            mine = by_core(me_x, z_bit)
            part = lax.dynamic_index_in_dim(halves, mine, 1, keepdims=False).reshape(-1, columns)
        for mask in far_masks:
            far, both = me_dp ^ mask, me_dp ^ mask ^ 1
            if token is None:
                near = dperm(part, mask)
                other = mixed(near, in_x, in_z)
                pieces += [near, other, dperm(near, 1), dperm(other, 1)]
                theirs = by_core(z_bit, me_x)
                places += [(far, mine), (far, 1 - mine), (both, theirs), (both, 1 - theirs)]
            else:
                near = held(dperm(shard, mask), token)
                pieces += [near, dperm(near, 1)]
                places += [(far, None), (both, None)]
        gathered, arrived = [], pieces[2]
        for i in range(number):
            moves, starts = [], []
            for j, (owner, which) in enumerate(places):
                size = count if which is None else half
                moves.append((j, i * size, size))
                starts.append(owner * count + (0 if which is None else which * half))
            gathered.append(assemble(pieces, moves, starts, n_dp * count))
        return gathered, arrived

    def split_masks():
        masks, mask = [], n_dp // 2
        while mask:
            masks.append(mask)
            mask //= 2
        return masks

    dp_masks = split_masks()

    def gather_tokens(value, token=None):
        for mask in dp_masks:
            got = dperm(value, mask)
            if token is not None and mask != 1:
                got = held(got, token)
            value = jnp.concatenate([value, got], axis=0)
        return value

    def scatter_tokens(value):
        for mask in reversed(dp_masks):
            half = value.shape[0] // 2
            value = value[:half] + dperm(value[half:].astype(BF), mask).astype(F32)
        return value

    def plus(left, right, *tokens):
        total = left.astype(F32) + right.astype(F32)
        for token in tokens:
            if token is not None:
                total = total + gate(token)
        return total.astype(BF)

    def joined_pair(part, other, axis):
        upper = me_x == 1
        pair = [jnp.where(upper, other, part), jnp.where(upper, part, other)]
        return jnp.concatenate(pair, axis=axis)

    def split_pair(value, axis, which):
        return (
            lax.dynamic_index_in_dim(value, which, axis, keepdims=False),
            lax.dynamic_index_in_dim(value, 1 - which, axis, keepdims=False),
        )

    def quarter_pair(own, token=None):
        pair = jnp.stack([own, mixed(own, in_z, in_x)])
        return pair if token is None else held(pair, token)

    def quarters_in_order(pair, axis, token):
        stack = jnp.concatenate([pair, held(mixed(pair, in_x, in_z), token)], axis=0)
        pieces = []
        for x in range(2):
            for z in range(2):
                rx, rz = me_x ^ x, z_bit ^ z
                pieces.append(at(stack, by_core(2 * rx + rz, 2 * rz + rx)))
        return jnp.concatenate(pieces, axis=axis).astype(F32)

    def far_along_z(value, token):
        mask = 2
        while mask < n_seq // 2:
            value = plus(value, zperm(value, mask), token)
            mask *= 2
        return value

    def shard_sums(blocks):
        number, (_, _, count, columns) = len(blocks), blocks[0].shape

        def side(which):
            size = (n_dp // 2, 1, count, columns)
            picked = [lax.dynamic_slice(b, (0, which, 0, 0), size) for b in blocks]
            return jnp.concatenate(picked, axis=1)

        mine, got = side(core), dperm(side(1 - core), 1)
        token = yield got
        size, mask, bits = n_dp // 2, n_dp // 4, me_dp >> 1
        while size > 2:
            mine, got = plus(mine, got, token), None
            here = bits & mask
            mine = mine.reshape((2, size // 2) + mine.shape[1:])
            keep, send = split_pair(mine, 0, jnp.where(here != 0, 1, 0))
            mine, got = keep, dperm(send, 2 * mask)
            size, mask = size // 2, mask // 2

        def block(which, first, second):
            far = far_bit ^ by_core(first, second)
            x = me_x ^ by_core(second, first)
            begin = (far, 0, x * (count // 2), 0)
            size = (1, number, count // 2, columns)
            return lax.dynamic_slice(which, begin, size)[0]

        def total(first, second):
            return plus(block(mine, first, second), block(got, first, second), token)

        sent = jnp.stack([total(1, 0), total(1, 1)])
        held_back = [total(0, 0), total(0, 1)]
        token = yield sent
        got = mixed(sent, in_far, in_x)
        send = plus(held_back[1], got[1], token)
        own = plus(held_back[0], got[0], token)
        token = yield send
        own = plus(own, mixed(send, in_x, in_far), token)
        size = (number, count // 4, columns)
        keep = lax.dynamic_slice(own, (0, z_bit * (count // 4), 0), size)
        send = lax.dynamic_slice(own, (0, (1 - z_bit) * (count // 4), 0), size)
        token = yield send
        own = plus(keep, zperm(send, 1), token)
        token = yield own
        own = far_along_z(own, token)
        token = yield own
        pair = quarter_pair(own, token)
        token = yield pair
        full = quarters_in_order(pair, 1, token)
        yield [full[i] for i in range(number)]

    def as_shards(grad):
        return grad.reshape((n_dp // 2, 2, -1) + grad.shape[1:])

    def sum_all(vector):
        for mask in dp_masks:
            vector = vector + dperm(vector, mask)
        vector = vector + xperm(vector)
        mask = 1
        while mask < n_seq // 2:
            vector = vector + zperm(vector, mask)
            mask *= 2
        return vector


    (skip_full,), _ = gather_weights([skip_weight])
    (qkv_full,), _ = gather_weights([qkv_weight])
    text_weight = text_kv_weight.reshape(text_kv_weight.shape[0], -1)
    text_count = text_weight.shape[0]
    text_pieces, text_marks = [text_weight], [0]
    for mask in dp_masks:
        text_pieces = text_pieces + [dperm(piece, mask) for piece in text_pieces]
        text_marks = text_marks + [mark ^ mask for mark in text_marks]
    text_weight = assemble(
        text_pieces,
        [(i, 0, text_count) for i in range(n_dp)],
        [(me_dp ^ mark) * text_count for mark in text_marks],
        n_dp * text_count,
    )
    text_weight = text_weight.reshape((-1,) + text_kv_weight.shape[1:])

    hidden_part = ffn_up_weight.shape[1] // n_dp
    up_rows = ffn_up_weight.shape[0]
    up_blocks = jnp.stack(
        [ffn_up_weight[:, i * hidden_part : (i + 1) * hidden_part] for i in range(n_dp)]
    )
    up_sends = [at(up_blocks, me_dp ^ mask) for mask in range(n_dp)]
    cot_rows = cotangent.reshape(rows, width)

    def gather_up(token):
        pieces = []
        for mask in range(n_dp):
            block = up_sends[mask]
            if mask:
                block = dperm(block, mask)
            pieces.append(held(block, token) if mask > 1 else block)
        return pieces[2:], assemble(
            pieces,
            [(i, 0, up_rows) for i in range(n_dp)],
            [(me_dp ^ mask) * up_rows for mask in range(n_dp)],
            n_dp * up_rows,
        )


    text_full = lax.all_gather(text_states, SEQ, axis=2, tiled=True)
    text_kv = jnp.einsum("che,bmc->bhem", text_weight, text_full, preferred_element_type=F32)
    tk_raw = text_kv[:, :, :HD]
    tk_mean, tk_rstd = norm_stats(tk_raw, -2)
    ck_gain = cross_key_gain[:, None]
    tkv_own = jnp.concatenate(
        [((tk_raw - tk_mean) * tk_rstd * ck_gain).astype(BF), text_kv[:, :, HD:].astype(BF)], axis=2
    )
    tkv_all = lax.all_gather(tkv_own, SEQ, axis=1, tiled=True)
    tk_all, tv_all = tkv_all[:, :, :HD], tkv_all[:, :, HD:]


    shift_rows = shift_weight.shape[0]
    all_steps = lax.dynamic_update_slice_in_dim(
        jnp.zeros((n_dp * batch,), F32), timesteps.astype(F32), me_dp * batch, axis=0
    )
    for mask in dp_masks:
        all_steps = all_steps + dperm(all_steps, mask)
    embed_all = jax.nn.silu(time_embed(all_steps, width)).astype(BF)
    embed_part = lax.dynamic_slice_in_dim(embed_all, me_dp * shift_rows, shift_rows, axis=1)
    shift_all = dot(embed_part, shift_weight, 1, 0)

    tables = rope_tables(positions)
    joined = jnp.concatenate([hidden_in, skip_in], axis=-1).reshape(rows, 2 * width).astype(F32)
    skip_mean, skip_rstd = norm_stats(joined, -1)
    skip_bf = ((joined - skip_mean) * skip_rstd * skip_gain).astype(BF)
    x1 = dot(skip_bf, skip_full, 1, 0) + gate(tkv_own) + sum(gate(b) for b in up_sends[1:])
    one_mean, one_rstd = norm_stats(x1, -1)
    for mask in reversed(dp_masks):
        shift_all = shift_all + dperm(shift_all, mask) + gate(x1)
    shift_vec = rows_at(shift_all, me_dp * batch, batch)
    shift_tokens = jnp.repeat(shift_vec, length, axis=0)
    first_bf = ((x1 - one_mean) * one_rstd * self_norm_gain + shift_tokens).astype(BF)
    qkv_raw = dot(qkv_full, first_bf, 0, 1).reshape(3, H, HD, rows)
    qk_gain = jnp.stack([query_gain, key_gain])[:, :, None]
    direct = length % 128 == 0

    def exchange(value):
        return lax.all_to_all(value, SEQ, split_axis=0, concat_axis=0, tiled=True)

    def to_heads(value):
        kinds = value.shape[2]
        value = exchange(value)
        if not direct:
            value = value.reshape(n_seq, group_heads, kinds, HD, batch, length)
            value = value.transpose(1, 2, 3, 4, 0, 5)
            value = value.reshape(1, group_heads, kinds, HD, batch * n_seq * length)
        return value

    def to_tokens(value):
        kinds = value.shape[2]
        if not direct:
            value = value.reshape(group_heads, kinds, HD, batch, n_seq, length)
            value = value.transpose(4, 0, 1, 2, 3, 5)
            value = value.reshape(n_seq, group_heads, kinds, HD, rows)
        return exchange(value)

    qkv = to_heads(qkv_norm_call(None, qkv_raw, qk_gain, tables, n_seq, "qkv_norm"))
    (self_out_full, cross_query_full, cross_out_full), out_arrived = gather_weights(
        [self_out_weight, cross_query_weight, cross_out_weight], qkv, x1
    )
    out, log_sum = attention_call(
        attend_forward_kernel, [qkv], batch, [1, 0], "attend_forward", pin_of(out_arrived)
    )
    self_tokens = to_tokens(out).reshape(width, rows)
    up_arrived, up_part = gather_up(out)
    cot_all = gather_tokens(cot_rows, self_tokens)
    x2 = x1 + dot(self_tokens, self_out_full, 0, 0) + sum(gate(p) for p in up_arrived)
    two_mean, two_rstd = norm_stats(x2, -1)
    second_bf = ((x2 - two_mean) * two_rstd * cross_norm_gain).astype(BF)

    cq_raw = dot(cross_query_full, second_bf, 0, 1).reshape(H, HD, rows)
    cq_mean, cq_rstd = norm_stats(cq_raw, -2)
    cq_gain = cross_query_gain[:, None]
    cq = ((cq_raw - cq_mean) * cq_rstd * cq_gain).astype(BF).reshape(H, HD, batch, length)
    cross_scores = SCALE * jnp.einsum("hebq,bhem->bhqm", cq, tk_all, preferred_element_type=F32)
    cross_max = jnp.max(cross_scores, axis=-1, keepdims=True)
    cross_exp = jnp.exp(cross_scores - cross_max)
    cross_probs = cross_exp / jnp.sum(cross_exp, axis=-1, keepdims=True)
    cross_probs_bf = cross_probs.astype(BF)
    cross_tokens = (
        jnp.einsum("bhqm,bhem->hebq", cross_probs_bf, tv_all, preferred_element_type=F32)
        .astype(BF)
        .reshape(width, rows)
    )
    x3 = x2 + dot(cross_tokens, cross_out_full, 0, 0)
    three_mean, three_rstd = norm_stats(x3, -1)
    third_bf = ((x3 - three_mean) * three_rstd * ffn_norm_gain).astype(BF)

    third_all = gather_tokens(third_bf)
    up = dot(up_part, third_all, 0, 1)
    active, gelu_pull = jax.vjp(lambda value: jax.nn.gelu(value, approximate=True), up)
    active_bf = active.astype(BF)
    grad_active = dot(ffn_down_weight, cot_all, 1, 1)
    grad_up = gelu_pull(grad_active)[0].astype(BF)
    grad_three_norm = scatter_tokens(dot(grad_up, up_part, 0, 1))
    block_out = x3 + scatter_tokens(dot(active_bf, ffn_down_weight, 0, 0))


    sub = hidden_part // 4

    def hidden_rows(value, first):
        pieces = []
        for second in range(2):
            x, z = me_x ^ by_core(first, second), z_bit ^ by_core(second, first)
            pieces.append(rows_at(value, (2 * x + z) * sub, sub))
        return jnp.concatenate(pieces, axis=0)

    def hidden_sums(left, right):
        sent = dot(hidden_rows(left, 1), right, 1, 0).astype(BF)
        kept = dot(hidden_rows(left, 0), right, 1, 0).astype(BF)
        token = yield sent
        got = mixed(sent, in_x, in_z)
        send = plus(kept[sub:], got[sub:], token)
        own = plus(kept[:sub], got[:sub], token)
        token = yield send
        own = plus(own, mixed(send, in_z, in_x), token)
        token = yield own
        own = far_along_z(own, token)
        token = yield own
        yield own if token is None else held(own, token)

    down = hidden_sums(active_bf, cot_all)
    up_back = hidden_sums(grad_up, third_all)
    first_sent = [next(down), next(up_back)]

    def up_pair(part, token):
        blocks = part.T.reshape(n_dp, up_rows, sub)
        own = [at(blocks, me_dp)] + [dperm(at(blocks, me_dp ^ m), m) for m in range(1, n_dp)]
        own = jnp.stack(own)
        return quarter_pair(jnp.stack([at(own, me_dp ^ i) for i in range(n_dp)]), token)


    grad_three_norm = grad_three_norm + (
        gate(first_sent[0]) + gate(first_sent[1]) + gate(up_back.send(None))
    )
    back_three, ffn_gain_rows = norm_back(
        grad_three_norm, x3, three_mean, three_rstd, ffn_norm_gain, -1
    )
    grad_three = cot_rows.astype(F32) + back_three
    grad_three_bf = grad_three.astype(BF)
    grad_cross = dot(cross_out_full, grad_three_bf, 1, 1).astype(BF).reshape(H, HD, batch, length)
    grad_cprobs = jnp.einsum("hebq,bhem->bhqm", grad_cross, tv_all, preferred_element_type=F32)
    cross_dot = jnp.sum(grad_cprobs * cross_probs, axis=-1, keepdims=True)
    grad_cscores = (cross_probs * (grad_cprobs - cross_dot)).astype(BF)
    grad_cq = (
        SCALE * jnp.einsum("bhqm,bhem->hebq", grad_cscores, tk_all, preferred_element_type=F32)
    ).astype(BF)
    grad_tk = SCALE * jnp.einsum("bhqm,hebq->hbem", grad_cscores, cq, preferred_element_type=F32)
    grad_tv = jnp.einsum("bhqm,hebq->hbem", cross_probs_bf, grad_cross, preferred_element_type=F32)
    grad_tkv = jnp.concatenate([grad_tk, grad_tv], axis=2).astype(BF)
    grad_tkv = grad_tkv.reshape((n_seq // 2, 2, group_heads) + grad_tkv.shape[1:])
    tkv_keep, tkv_send = split_pair(grad_tkv, 1, me_x)
    tkv_got = xperm(tkv_send)

    sent = gate(up_back.send(grad_three_bf)) + gate(down.send(grad_three_bf))
    back_cq, cq_gain_rows = norm_back(
        grad_cq.reshape(H, HD, rows).astype(F32), cq_raw, cq_mean, cq_rstd, cq_gain + sent, -2
    )
    grad_cq_raw = back_cq.astype(BF).reshape(width, rows)
    grad_two_norm = dot(grad_cq_raw, cross_query_full, 0, 1)
    sent = gate(down.send(grad_cq_raw))
    back_two, cross_gain_rows = norm_back(
        grad_two_norm, x2, two_mean, two_rstd, cross_norm_gain + sent, -1
    )
    grad_two = grad_three + back_two
    grad_two_bf = grad_two.astype(BF)
    middle = shard_sums(
        [
            as_shards(dot(cross_tokens, grad_three_bf, 1, 0).astype(BF)),
            as_shards(dot(second_bf, grad_cq_raw, 0, 1).astype(BF)),
            as_shards(dot(self_tokens, grad_two_bf, 1, 0).astype(BF)),
        ]
    )
    next(middle)
    grad_out = dot(self_out_full, grad_two_bf, 1, 1).astype(BF)
    grad_out = to_heads(grad_out.reshape(n_seq, group_heads, 1, HD, rows))
    pin = pin_of(middle.send(grad_two_bf))
    (grad_heads,) = attention_call(
        attend_backward_kernel, [qkv, log_sum, grad_out], batch, [3], "attend_backward", pin
    )
    grad_tokens = to_tokens(grad_heads)
    middle_x = middle.send(grad_heads)
    back_qkv, qk_gain_sum = qkv_norm_call(
        grad_tokens, qkv_raw, qk_gain + gate(middle_x), tables, n_seq, "qkv_norm_back"
    )
    back_qkv = back_qkv.reshape(3 * width, rows)
    late = shard_sums([as_shards(dot(first_bf, back_qkv, 0, 1).astype(BF))])
    next(late)
    grad_one_norm = dot(back_qkv, qkv_full, 0, 1)
    middle_z = middle.send(back_qkv)
    late_far = late.send(back_qkv)
    grad_one_norm = grad_one_norm + (gate(middle_z) + gate(late_far))
    shift_part = jnp.sum(grad_one_norm.reshape(batch, length, width), axis=1)
    back_one, self_gain_rows = norm_back(
        grad_one_norm, x1, one_mean, one_rstd, self_norm_gain, -1
    )
    grad_one_bf = (grad_two + back_one).astype(BF)
    skip_blocks = dot(skip_bf, grad_one_bf, 0, 0).astype(BF)
    skip_blocks = skip_blocks.reshape(n_dp // 2, 2, 2, -1, width)
    end = shard_sums([skip_blocks[:, :, i] for i in range(2)])
    next(end)
    grad_skip_norm = dot(grad_one_bf, skip_full, 1, 1)
    grad_tkv = plus(tkv_keep, tkv_got, grad_one_bf)
    grad_tkv = lax.psum_scatter(grad_tkv, "z", scatter_dimension=0, tiled=True)
    middle_z = middle.send(grad_one_bf)
    back_joined, skip_gain_rows = norm_back(
        grad_skip_norm, joined, skip_mean, skip_rstd, skip_gain + gate(middle_z), -1
    )

    steps = [grad_one_bf]

    def then(value):
        steps.append(value[0] if isinstance(value, list) else value)
        return value

    def step(sums):
        return then(sums.send(steps[-1]))

    step(down)
    down_own = down.send(None)
    step(end)
    step(late)
    down_pair = then(quarter_pair(down_own, steps[-1]))
    step(up_back)
    up_own = up_back.send(None)
    step(end)
    step(middle)
    step(late)
    up_grad_pair = then(up_pair(up_own, steps[-1]))
    step(end)
    step(middle)
    step(late)
    down_grad = then(quarters_in_order(down_pair, 0, steps[-1]))
    step(end)
    up_grad = then(quarters_in_order(up_grad_pair, 2, steps[-1]))
    up_grad = up_grad.transpose(1, 0, 2).reshape(up_rows, -1)
    step(late)
    cross_out_grad, cross_query_grad, self_out_grad = step(middle)
    step(end)
    step(late)
    step(end)
    (qkv_grad,) = step(late)
    skip_parts = step(end)
    skip_grad_w = jnp.concatenate(skip_parts, axis=0)
    back_joined = back_joined.astype(BF).reshape(batch, length, 2 * width)


    grad_tkv = grad_tkv.reshape(grad_tkv.shape[1:]).astype(F32) + gate(steps[8])
    grad_tkv = grad_tkv.swapaxes(0, 1)
    back_tk, ck_gain_rows = norm_back(
        grad_tkv[:, :, :HD], tk_raw, tk_mean, tk_rstd, ck_gain, -2
    )
    grad_tkv_bf = jnp.concatenate([back_tk, grad_tkv[:, :, HD:]], axis=2).astype(BF)
    text_kv_grad = jnp.einsum("bmc,bhem->che", text_full, grad_tkv_bf, preferred_element_type=F32)
    text_part = jnp.einsum("bhem,che->cbm", grad_tkv_bf, text_weight, preferred_element_type=F32)
    text_part = text_part.astype(BF).reshape(n_seq // 2, 2, -1, batch * text_len)
    text_keep, text_send = split_pair(text_part, 1, me_x)
    text_part = plus(text_keep, xperm(text_send))
    text_grad = lax.psum_scatter(text_part, "z", scatter_dimension=0, tiled=True)
    text_grad = text_grad.reshape(-1, batch, text_len).transpose(1, 2, 0)
    text_kv_grad = text_kv_grad.astype(BF).reshape(n_dp // 2, 2, text_count, -1)
    text_keep, text_send = split_pair(text_kv_grad, 1, me_dp & 1)
    text_own = plus(text_keep, dperm(text_send, 1))
    text_kv_sum = at(text_own, me_dp >> 1)
    for mask in far_masks:
        text_kv_sum = plus(text_kv_sum, dperm(at(text_own, (me_dp ^ mask) >> 1), mask))
    text_kv_sum = text_kv_sum.astype(F32).reshape(text_kv_weight.shape)


    shift_slots = lax.dynamic_update_slice_in_dim(
        jnp.zeros((n_dp * batch, width), F32), shift_part, me_dp * batch, axis=0
    )
    vectors = [
        jnp.sum(ffn_gain_rows, axis=0),
        jnp.sum(cross_gain_rows, axis=0),
        jnp.sum(self_gain_rows, axis=0),
        qk_gain_sum[0, :, 0],
        qk_gain_sum[1, :, 0],
        jnp.sum(cq_gain_rows, axis=(0, 2)),
        jnp.sum(ck_gain_rows, axis=(0, 1, 3)),
        shift_slots.reshape(-1),
    ]
    vectors.append(jnp.sum(skip_gain_rows, axis=0))
    total = sum_all(jnp.concatenate(vectors))
    sums, start = [], 0
    for vector in vectors:
        sums.append(total[start : start + vector.shape[0]])
        start += vector.shape[0]
    ffn_gain, cross_gain, self_gain, q_gain_all, k_gain_all, cq_gain_sum, ck_gain_sum = sums[:7]
    shift_total, skip_gain_sum = sums[7:]
    shift_grad = lax.dot_general(
        embed_part.astype(F32),
        shift_total.reshape(n_dp * batch, width),
        (((0,), (0,)), ((), ())),
        precision=lax.Precision.HIGHEST,
        preferred_element_type=F32,
    )

    return (
        block_out.astype(BF).reshape(batch, length, width),
        back_joined[..., :width],
        back_joined[..., width:],
        text_grad,
        skip_gain_sum,
        skip_grad_w,
        self_gain,
        shift_grad,
        qkv_grad,
        q_gain_all,
        k_gain_all,
        self_out_grad,
        cross_gain,
        cross_query_grad,
        text_kv_sum,
        cq_gain_sum,
        ck_gain_sum,
        cross_out_grad,
        ffn_gain,
        up_grad,
        down_grad,
    )


def solution(mesh):
    n_dp, n_seq = mesh.shape["dp"], mesh.shape["seq"]
    mesh = Mesh(mesh.devices.reshape(n_dp, n_seq // 2, 2), ("dp", "z", "x"))
    tokens, text, rows, none = P("dp", SEQ, None), P("dp", None, SEQ), P("dp", None), P()
    heads = P("dp", SEQ, None)
    placed = (
        tokens, tokens, text, P("dp"), text, tokens, none, rows, none, rows, rows, none, none,
        rows, none, rows, heads, none, none, rows, none, rows, rows,
    )
    given = (
        tokens, tokens, tokens, text, none, rows, none, rows, rows, none, none, rows, none, rows,
        heads, none, none, rows, none, rows, rows,
    )
    return jax.shard_map(local, mesh=mesh, in_specs=placed, out_specs=given, check_vma=False)
```

```python
import math

import jax
import jax.numpy as jnp
from jax import lax
from jax.experimental import pallas as pl
from jax.experimental.pallas import tpu as pltpu
from jax.sharding import Mesh, PartitionSpec as P

H = 16
HD = 88
SCALE = HD ** (-0.5)
norm_eps = 1e-06
F32 = jnp.float32
BF = jnp.bfloat16
SEQ = ("z", "x")
SMALL = pl.CostEstimate(flops=1024, bytes_accessed=1024, transcendentals=0)


def dot(left, right, left_dim, right_dim):
    return lax.dot_general(
        left, right, (((left_dim,), (right_dim,)), ((), ())), preferred_element_type=F32
    )


def norm_stats(tensor, axis):
    mean = jnp.mean(tensor, axis=axis, keepdims=True)
    center = tensor - mean
    spread = jnp.mean(center * center, axis=axis, keepdims=True)
    return mean, lax.rsqrt(spread + norm_eps)


def norm_back(grad, tensor, mean, rstd, gain, axis):
    normed = (tensor - mean) * rstd
    scaled = grad * gain
    first = jnp.mean(scaled, axis=axis, keepdims=True)
    second = jnp.mean(scaled * normed, axis=axis, keepdims=True)
    return rstd * (scaled - first - normed * second), grad * normed


def time_embed(step_ids, embed_width):
    half_width = embed_width // 2
    frequency = jnp.exp(-math.log(10000.0) * jnp.arange(half_width, dtype=F32) / half_width)
    angles = step_ids.astype(F32)[:, None] * frequency[None, :]
    return jnp.concatenate([jnp.cos(angles), jnp.sin(angles)], axis=-1)


def rope_tables(grid_pos):
    quarter = HD // 4
    frequency = jnp.exp(-math.log(10000.0) * jnp.arange(quarter, dtype=F32) / quarter)
    row = frequency[:, None] * grid_pos[:, 0, :].astype(F32).reshape(1, -1)
    col = frequency[:, None] * grid_pos[:, 1, :].astype(F32).reshape(1, -1)
    nil = jnp.zeros_like(row)
    cos_row, sin_row, cos_col, sin_col = jnp.cos(row), jnp.sin(row), jnp.cos(col), jnp.sin(col)
    own = jnp.concatenate([cos_row, cos_row, cos_col, cos_col], axis=0)
    upper = jnp.concatenate([-sin_row, nil, -sin_col, nil], axis=0)
    lower = jnp.concatenate([nil, sin_row, nil, sin_col], axis=0)
    return own, upper, lower


def qkv_norm_kernel(raw_ref, gain_ref, own_ref, upper_ref, lower_ref, out_ref):
    quarter = HD // 4
    for i in range(raw_ref.shape[1]):
        for kind in range(2):
            raw = raw_ref[kind, i]
            mean, rstd = norm_stats(raw, 0)
            value = (raw - mean) * rstd * gain_ref[kind]
            value = (
                value * own_ref[...]
                + pltpu.roll(value, HD - quarter, 0) * upper_ref[...]
                + pltpu.roll(value, quarter, 0) * lower_ref[...]
            )
            out_ref[0, i, kind] = value.astype(BF)
        out_ref[0, i, 2] = raw_ref[2, i].astype(BF)


def qkv_norm_back_kernel(
    grad_ref, raw_ref, gain_ref, own_ref, upper_ref, lower_ref, out_ref, sum_ref
):
    quarter = HD // 4

    @pl.when(pl.program_id(0) == 0)
    def _():
        sum_ref[...] = jnp.zeros_like(sum_ref)

    for i in range(raw_ref.shape[1]):
        for kind in range(2):
            grad = grad_ref[0, i, kind].astype(F32)
            grad = (
                grad * own_ref[...]
                + pltpu.roll(grad * upper_ref[...], quarter, 0)
                + pltpu.roll(grad * lower_ref[...], HD - quarter, 0)
            )
            raw = raw_ref[kind, i]
            mean, rstd = norm_stats(raw, 0)
            back, part = norm_back(grad, raw, mean, rstd, gain_ref[kind], 0)
            out_ref[kind, i] = back.astype(BF)
            sum_ref[kind] += jnp.sum(part, axis=1, keepdims=True)
        out_ref[2, i] = grad_ref[0, i, 2]


def qkv_norm_call(grads, raw, gains, tables, groups, name):
    kinds, heads, features, tokens = raw.shape
    own = heads // groups
    by_kind = pl.BlockSpec((kinds, own, features, tokens), lambda i: (0, i, 0, 0))
    by_group = pl.BlockSpec((1, own, kinds, features, tokens), lambda i: (i, 0, 0, 0, 0))
    table = pl.BlockSpec((features, tokens), lambda i: (0, 0))
    column = pl.BlockSpec((2, features, 1), lambda i: (0, 0, 0))
    group_shape = jax.ShapeDtypeStruct((groups, own, kinds, features, tokens), BF)
    kind_shape = jax.ShapeDtypeStruct(raw.shape, BF)
    total = jax.ShapeDtypeStruct((2, features, 1), F32)
    back = grads is not None
    return pl.pallas_call(
        qkv_norm_back_kernel if back else qkv_norm_kernel,
        grid=(groups,),
        in_specs=([by_group] if back else []) + [by_kind, column] + [table] * 3,
        out_specs=[by_kind, column] if back else by_group,
        out_shape=[kind_shape, total] if back else group_shape,
        compiler_params=pltpu.CompilerParams(vmem_limit_bytes=32 * 2**20),
        cost_estimate=SMALL,
        name=name,
    )(*([grads] if back else []), raw, gains, *tables)


def gate(value):
    corner = value[(0,) * value.ndim].astype(F32)
    return jnp.where(corner != corner, 1.0, 0.0)


def pin_of(*values):
    return jnp.zeros((8, 128), F32) + sum(gate(value) for value in values)


def assemble_kernel(count, moves, starts, *refs):
    pieces, out, sems = refs[:count], refs[count], refs[count + 1]
    copies = [
        pltpu.make_async_copy(
            pieces[piece].at[pl.ds(source, size)],
            out.at[pl.ds(pl.multiple_of(starts[i], 16), size)],
            sems.at[i],
        )
        for i, (piece, source, size) in enumerate(moves)
    ]
    for copy in copies:
        copy.start()
    for copy in copies:
        copy.wait()


def assemble(pieces, moves, starts, rows):
    columns, dtype = pieces[0].shape[1], pieces[0].dtype
    if columns % 128 or any(source % 16 or size % 16 for _, source, size in moves):
        full = jnp.zeros((rows, columns), dtype)
        for (piece, source, size), start in zip(moves, starts):
            block = pieces[piece][source : source + size]
            full = lax.dynamic_update_slice_in_dim(full, block, start, axis=0)
        return full
    count = len(pieces)
    anywhere = pl.BlockSpec(memory_space=pl.ANY)

    def kernel(starts_ref, *refs):
        assemble_kernel(count, moves, starts_ref, *refs)

    return pl.pallas_call(
        kernel,
        out_shape=jax.ShapeDtypeStruct((rows, columns), dtype),
        grid_spec=pltpu.PrefetchScalarGridSpec(
            num_scalar_prefetch=1,
            grid=(1,),
            in_specs=[anywhere] * count,
            out_specs=pl.BlockSpec(memory_space=pltpu.VMEM),
            scratch_shapes=[pltpu.SemaphoreType.DMA((len(moves),))],
        ),
        compiler_params=pltpu.CompilerParams(vmem_limit_bytes=32 * 2**20),
        cost_estimate=SMALL,
        name="assemble",
    )(jnp.stack([jnp.asarray(start, jnp.int32) for start in starts]), *pieces)


def wide(ref, kind, first, count):
    return jnp.concatenate([ref[first + i, 0, kind] for i in range(count)], axis=1)


def contract(left, right, left_dim, right_dim):
    return lax.dot_general(
        left, right, (((left_dim,), (right_dim,)), ((), ())), preferred_element_type=F32
    )


def attend_forward_kernel(step, qkv_ref, pin_ref, out_ref, log_ref):
    blocks, lanes = qkv_ref.shape[0], qkv_ref.shape[4]
    k, v = wide(qkv_ref, 1, 0, blocks), wide(qkv_ref, 2, 0, blocks)
    for first in range(0, blocks, step):
        q = wide(qkv_ref, 0, first, step)
        scores = SCALE * contract(k, q, 0, 0)
        top = jnp.max(scores, axis=0, keepdims=True)
        weights = jnp.exp(scores - top)
        total = jnp.sum(weights, axis=0, keepdims=True)
        out = contract(v, weights.astype(BF), 1, 0) / total
        log_ref[0, 0, :, first * lanes : (first + step) * lanes] = top + jnp.log(total)
        for i in range(step):
            out_ref[first + i, 0, 0] = out[:, i * lanes : (i + 1) * lanes].astype(BF)


def attend_backward_kernel(step, qkv_ref, log_ref, g_ref, pin_ref, out_ref):
    blocks, lanes = qkv_ref.shape[0], qkv_ref.shape[4]
    k, v = wide(qkv_ref, 1, 0, blocks), wide(qkv_ref, 2, 0, blocks)
    dk = jnp.zeros((k.shape[0], k.shape[1]), F32)
    dv = dk
    for first in range(0, blocks, step):
        q, g = wide(qkv_ref, 0, first, step), wide(g_ref, 0, first, step)
        log_sum = log_ref[0, 0, :, first * lanes : (first + step) * lanes]
        probs = jnp.exp(SCALE * contract(k, q, 0, 0) - log_sum)
        grad_probs = contract(v, g, 0, 0)
        delta = jnp.sum(grad_probs * probs, axis=0, keepdims=True)
        grad_scores = (probs * (grad_probs - delta)).astype(BF)
        dq = SCALE * contract(k, grad_scores, 1, 0)
        dk = dk + contract(q, grad_scores, 1, 1)
        dv = dv + contract(g, probs.astype(BF), 1, 1)
        for i in range(step):
            out_ref[first + i, 0, 0] = dq[:, i * lanes : (i + 1) * lanes].astype(BF)
    for i in range(blocks):
        out_ref[i, 0, 1] = (SCALE * dk[:, i * lanes : (i + 1) * lanes]).astype(BF)
        out_ref[i, 0, 2] = dv[:, i * lanes : (i + 1) * lanes].astype(BF)


def attention_call(kernel, arrays, batch, made, name, pin):
    blocks, heads, _, _, lanes = arrays[0].shape
    lanes //= batch

    def spec(kinds):
        if kinds:
            return pl.BlockSpec((blocks, 1, kinds, HD, lanes), lambda b, h: (0, h, 0, 0, b))
        return pl.BlockSpec((1, 1, 1, blocks * lanes), lambda b, h: (b, h, 0, 0))

    def shape(kinds):
        if kinds:
            return jax.ShapeDtypeStruct((blocks, heads, kinds, HD, batch * lanes), BF)
        return jax.ShapeDtypeStruct((batch, heads, 1, blocks * lanes), F32)

    step = max(1, min(blocks, 256 // lanes))
    body = lambda *refs: kernel(step, *refs)
    return pl.pallas_call(
        body,
        grid=(batch, heads),
        in_specs=[spec(a.shape[2] if a.ndim == 5 else 0) for a in arrays]
        + [pl.BlockSpec((8, 128), lambda b, h: (0, 0))],
        out_specs=[spec(kinds) for kinds in made],
        out_shape=[shape(kinds) for kinds in made],
        compiler_params=pltpu.CompilerParams(vmem_limit_bytes=48 * 2**20),
        cost_estimate=SMALL,
        name=name,
    )(*arrays, pin)


def local(
    hidden_in,
    skip_in,
    text_states,
    timesteps,
    positions,
    cotangent,
    skip_gain,
    skip_weight,
    self_norm_gain,
    shift_weight,
    qkv_weight,
    query_gain,
    key_gain,
    self_out_weight,
    cross_norm_gain,
    cross_query_weight,
    text_kv_weight,
    cross_query_gain,
    cross_key_gain,
    cross_out_weight,
    ffn_norm_gain,
    ffn_up_weight,
    ffn_down_weight,
):
    n_dp, n_seq = lax.axis_size("dp"), lax.axis_size(SEQ)
    me_dp, me_x = lax.axis_index("dp"), lax.axis_index("x")
    batch, length, width = hidden_in.shape
    rows = batch * length
    group_heads = H // n_seq
    text_len = text_states.shape[1]


    def dperm(value, mask):
        return lax.ppermute(value, "dp", [(i, i ^ mask) for i in range(n_dp)])

    def xperm(value):
        return lax.ppermute(value, "x", [(0, 1), (1, 0)])

    def zperm(value, mask):
        return lax.ppermute(value, "z", [(i, i ^ mask) for i in range(n_seq // 2)])

    def mixed(value, first, second):
        sizes = {"dp": n_dp, "z": n_seq // 2, "x": 2}

        def number(place):
            return (place["dp"] * sizes["z"] + place["z"]) * 2 + place["x"]

        pairs = []
        for d in range(n_dp):
            for z in range(sizes["z"]):
                for x in range(2):
                    place = {"dp": d, "z": z, "x": x}
                    axis, mask = second if d & 1 else first
                    pairs.append((number(place), number({**place, axis: place[axis] ^ mask})))
        return lax.ppermute(value, ("dp", "z", "x"), pairs)

    core, far_bit = me_dp & 1, (me_dp >> 1) & 1
    z_bit = lax.axis_index("z") & 1
    in_z, in_x, in_far = ("z", 1), ("x", 1), ("dp", 2)

    def by_core(first, second):
        return jnp.where(core == 1, second, first)

    def rows_at(value, start, count):
        return lax.dynamic_slice_in_dim(value, start, count, axis=0)

    def at(value, place):
        return lax.dynamic_index_in_dim(value, place, 0, keepdims=False)

    far_masks = list(range(2, n_dp, 2))

    def held(value, token):
        return (value.astype(F32) + gate(token)).astype(value.dtype)

    def gather_weights(shards, token=None, start=None):
        number, (count, columns) = len(shards), shards[0].shape
        half = count // 2
        shard = jnp.concatenate(shards, axis=0) if number > 1 else shards[0]
        if start is not None:
            shard = held(shard, start)
        pieces, places = [shard, dperm(shard, 1)], [(me_dp, None), (me_dp ^ 1, None)]
        if token is None:
            halves = shard.reshape(number, 2, half, columns)
            mine = by_core(me_x, z_bit)
            part = lax.dynamic_index_in_dim(halves, mine, 1, keepdims=False).reshape(-1, columns)
        for mask in far_masks:
            far, both = me_dp ^ mask, me_dp ^ mask ^ 1
            if token is None:
                near = dperm(part, mask)
                other = mixed(near, in_x, in_z)
                pieces += [near, other, dperm(near, 1), dperm(other, 1)]
                theirs = by_core(z_bit, me_x)
                places += [(far, mine), (far, 1 - mine), (both, theirs), (both, 1 - theirs)]
            else:
                near = held(dperm(shard, mask), token)
                pieces += [near, dperm(near, 1)]
                places += [(far, None), (both, None)]
        gathered, arrived = [], pieces[2]
        for i in range(number):
            moves, starts = [], []
            for j, (owner, which) in enumerate(places):
                size = count if which is None else half
                moves.append((j, i * size, size))
                starts.append(owner * count + (0 if which is None else which * half))
            gathered.append(assemble(pieces, moves, starts, n_dp * count))
        return gathered, arrived

    def split_masks():
        masks, mask = [], n_dp // 2
        while mask:
            masks.append(mask)
            mask //= 2
        return masks

    dp_masks = split_masks()

    def gather_tokens(value, token=None):
        for mask in dp_masks:
            got = dperm(value, mask)
            if token is not None and mask != 1:
                got = held(got, token)
            value = jnp.concatenate([value, got], axis=0)
        return value

    def scatter_tokens(value):
        for mask in reversed(dp_masks):
            half = value.shape[0] // 2
            value = value[:half] + dperm(value[half:].astype(BF), mask).astype(F32)
        return value

    def plus(left, right, *tokens):
        total = left.astype(F32) + right.astype(F32)
        for token in tokens:
            if token is not None:
                total = total + gate(token)
        return total.astype(BF)

    def joined_pair(part, other, axis):
        upper = me_x == 1
        pair = [jnp.where(upper, other, part), jnp.where(upper, part, other)]
        return jnp.concatenate(pair, axis=axis)

    def split_pair(value, axis, which):
        return (
            lax.dynamic_index_in_dim(value, which, axis, keepdims=False),
            lax.dynamic_index_in_dim(value, 1 - which, axis, keepdims=False),
        )

    def quarter_pair(own, token=None):
        pair = jnp.stack([own, mixed(own, in_z, in_x)])
        return pair if token is None else held(pair, token)

    def quarters_in_order(pair, axis, token):
        stack = jnp.concatenate([pair, held(mixed(pair, in_x, in_z), token)], axis=0)
        pieces = []
        for x in range(2):
            for z in range(2):
                rx, rz = me_x ^ x, z_bit ^ z
                pieces.append(at(stack, by_core(2 * rx + rz, 2 * rz + rx)))
        return jnp.concatenate(pieces, axis=axis).astype(F32)

    def far_along_z(value, token):
        mask = 2
        while mask < n_seq // 2:
            value = plus(value, zperm(value, mask), token)
            mask *= 2
        return value

    def shard_sums(blocks, joined=False):
        number, (_, _, count, columns) = len(blocks), blocks[0].shape

        def side(which):
            size = (n_dp // 2, 1, count, columns)
            picked = [lax.dynamic_slice(b, (0, which, 0, 0), size) for b in blocks]
            return jnp.concatenate(picked, axis=1)

        mine, got = side(core), dperm(side(1 - core), 1)
        token = yield got
        size, mask, bits = n_dp // 2, n_dp // 4, me_dp >> 1
        while size > 2:
            mine, got = plus(mine, got, token), None
            here = bits & mask
            mine = mine.reshape((2, size // 2) + mine.shape[1:])
            keep, send = split_pair(mine, 0, jnp.where(here != 0, 1, 0))
            mine, got = keep, dperm(send, 2 * mask)
            size, mask = size // 2, mask // 2

        def block(which, first, second):
            far = far_bit ^ by_core(first, second)
            x = me_x ^ by_core(second, first)
            begin = (far, 0, x * (count // 2), 0)
            size = (1, number, count // 2, columns)
            return lax.dynamic_slice(which, begin, size)[0]

        def total(first, second):
            return plus(block(mine, first, second), block(got, first, second), token)

        sent = jnp.stack([total(1, 0), total(1, 1)])
        held_back = [total(0, 0), total(0, 1)]
        token = yield sent
        got = mixed(sent, in_far, in_x)
        send = plus(held_back[1], got[1], token)
        own = plus(held_back[0], got[0], token)
        token = yield send
        own = plus(own, mixed(send, in_x, in_far), token)
        size = (number, count // 4, columns)
        keep = lax.dynamic_slice(own, (0, z_bit * (count // 4), 0), size)
        send = lax.dynamic_slice(own, (0, (1 - z_bit) * (count // 4), 0), size)
        token = yield send
        own = plus(keep, zperm(send, 1), token)
        token = yield own
        own = far_along_z(own, token)
        token = yield own
        pair = quarter_pair(own, token)
        token = yield pair
        full = quarters_in_order(pair, 1, token)
        yield [full.reshape(-1, columns)] if joined else [full[i] for i in range(number)]

    def as_shards(grad):
        return grad.reshape((n_dp // 2, 2, -1) + grad.shape[1:])

    def sum_all(vector):
        for mask in dp_masks:
            vector = vector + dperm(vector, mask)
        vector = vector + xperm(vector)
        mask = 1
        while mask < n_seq // 2:
            vector = vector + zperm(vector, mask)
            mask *= 2
        return vector


    (skip_full,), _ = gather_weights([skip_weight])
    (qkv_full,), _ = gather_weights([qkv_weight])
    text_weight = text_kv_weight.reshape(text_kv_weight.shape[0], -1)
    text_count = text_weight.shape[0]
    text_pieces, text_marks = [text_weight], [0]
    for mask in dp_masks:
        text_pieces = text_pieces + [dperm(piece, mask) for piece in text_pieces]
        text_marks = text_marks + [mark ^ mask for mark in text_marks]
    text_weight = assemble(
        text_pieces,
        [(i, 0, text_count) for i in range(n_dp)],
        [(me_dp ^ mark) * text_count for mark in text_marks],
        n_dp * text_count,
    )
    text_weight = text_weight.reshape((-1,) + text_kv_weight.shape[1:])

    hidden_part = ffn_up_weight.shape[1] // n_dp
    up_rows = ffn_up_weight.shape[0]
    up_blocks = jnp.stack(
        [ffn_up_weight[:, i * hidden_part : (i + 1) * hidden_part] for i in range(n_dp)]
    )
    up_sends = [at(up_blocks, me_dp ^ mask) for mask in range(n_dp)]
    cot_rows = cotangent.reshape(rows, width)

    def gather_up(token):
        pieces = []
        for mask in range(n_dp):
            block = up_sends[mask]
            if mask:
                block = dperm(block, mask)
            pieces.append(held(block, token) if mask > 1 else block)
        return pieces[2:], assemble(
            pieces,
            [(i, 0, up_rows) for i in range(n_dp)],
            [(me_dp ^ mask) * up_rows for mask in range(n_dp)],
            n_dp * up_rows,
        )


    text_full = lax.all_gather(text_states, SEQ, axis=2, tiled=True)
    text_kv = jnp.einsum("che,bmc->bhem", text_weight, text_full, preferred_element_type=F32)
    tk_raw = text_kv[:, :, :HD]
    tk_mean, tk_rstd = norm_stats(tk_raw, -2)
    ck_gain = cross_key_gain[:, None]
    tkv_own = jnp.concatenate(
        [((tk_raw - tk_mean) * tk_rstd * ck_gain).astype(BF), text_kv[:, :, HD:].astype(BF)], axis=2
    )
    tkv_all = lax.all_gather(tkv_own, SEQ, axis=1, tiled=True)
    tk_all, tv_all = tkv_all[:, :, :HD], tkv_all[:, :, HD:]


    shift_rows = shift_weight.shape[0]
    all_steps = lax.dynamic_update_slice_in_dim(
        jnp.zeros((n_dp * batch,), F32), timesteps.astype(F32), me_dp * batch, axis=0
    )
    for mask in dp_masks:
        all_steps = all_steps + dperm(all_steps, mask)
    embed_all = jax.nn.silu(time_embed(all_steps, width)).astype(BF)
    embed_part = lax.dynamic_slice_in_dim(embed_all, me_dp * shift_rows, shift_rows, axis=1)
    shift_all = dot(embed_part, shift_weight, 1, 0)

    tables = rope_tables(positions)
    joined = jnp.concatenate([hidden_in, skip_in], axis=-1).reshape(rows, 2 * width).astype(F32)
    skip_mean, skip_rstd = norm_stats(joined, -1)
    skip_bf = ((joined - skip_mean) * skip_rstd * skip_gain).astype(BF)
    x1 = dot(skip_bf, skip_full, 1, 0) + gate(tkv_own) + sum(gate(b) for b in up_sends[1:])
    one_mean, one_rstd = norm_stats(x1, -1)
    for mask in reversed(dp_masks):
        shift_all = shift_all + dperm(shift_all, mask) + gate(x1)
    shift_vec = rows_at(shift_all, me_dp * batch, batch)
    shift_tokens = jnp.repeat(shift_vec, length, axis=0)
    first_bf = ((x1 - one_mean) * one_rstd * self_norm_gain + shift_tokens).astype(BF)
    qkv_raw = dot(qkv_full, first_bf, 0, 1).reshape(3, H, HD, rows)
    qk_gain = jnp.stack([query_gain, key_gain])[:, :, None]
    direct = length % 128 == 0

    def exchange(value):
        return lax.all_to_all(value, SEQ, split_axis=0, concat_axis=0, tiled=True)

    def to_heads(value):
        kinds = value.shape[2]
        value = exchange(value)
        if not direct:
            value = value.reshape(n_seq, group_heads, kinds, HD, batch, length)
            value = value.transpose(1, 2, 3, 4, 0, 5)
            value = value.reshape(1, group_heads, kinds, HD, batch * n_seq * length)
        return value

    def to_tokens(value):
        kinds = value.shape[2]
        if not direct:
            value = value.reshape(group_heads, kinds, HD, batch, n_seq, length)
            value = value.transpose(4, 0, 1, 2, 3, 5)
            value = value.reshape(n_seq, group_heads, kinds, HD, rows)
        return exchange(value)

    qkv = to_heads(qkv_norm_call(None, qkv_raw, qk_gain, tables, n_seq, "qkv_norm"))
    (self_out_full, cross_query_full, cross_out_full), out_arrived = gather_weights(
        [self_out_weight, cross_query_weight, cross_out_weight], qkv, x1
    )
    out, log_sum = attention_call(
        attend_forward_kernel, [qkv], batch, [1, 0], "attend_forward", pin_of(out_arrived)
    )
    self_tokens = to_tokens(out).reshape(width, rows)
    up_arrived, up_part = gather_up(out)
    cot_all = gather_tokens(cot_rows, self_tokens)
    x2 = x1 + dot(self_tokens, self_out_full, 0, 0) + sum(gate(p) for p in up_arrived)
    two_mean, two_rstd = norm_stats(x2, -1)
    second_bf = ((x2 - two_mean) * two_rstd * cross_norm_gain).astype(BF)

    cq_raw = dot(cross_query_full, second_bf, 0, 1).reshape(H, HD, rows)
    cq_mean, cq_rstd = norm_stats(cq_raw, -2)
    cq_gain = cross_query_gain[:, None]
    cq = ((cq_raw - cq_mean) * cq_rstd * cq_gain).astype(BF).reshape(H, HD, batch, length)
    cross_scores = SCALE * jnp.einsum("hebq,bhem->bhqm", cq, tk_all, preferred_element_type=F32)
    cross_max = jnp.max(cross_scores, axis=-1, keepdims=True)
    cross_exp = jnp.exp(cross_scores - cross_max)
    cross_probs = cross_exp / jnp.sum(cross_exp, axis=-1, keepdims=True)
    cross_probs_bf = cross_probs.astype(BF)
    cross_tokens = (
        jnp.einsum("bhqm,bhem->hebq", cross_probs_bf, tv_all, preferred_element_type=F32)
        .astype(BF)
        .reshape(width, rows)
    )
    x3 = x2 + dot(cross_tokens, cross_out_full, 0, 0)
    three_mean, three_rstd = norm_stats(x3, -1)
    third_bf = ((x3 - three_mean) * three_rstd * ffn_norm_gain).astype(BF)

    third_all = gather_tokens(third_bf)
    up = dot(up_part, third_all, 0, 1)
    active, gelu_pull = jax.vjp(lambda value: jax.nn.gelu(value, approximate=True), up)
    active_bf = active.astype(BF)
    grad_active = dot(ffn_down_weight, cot_all, 1, 1)
    grad_up = gelu_pull(grad_active)[0].astype(BF)
    grad_three_norm = scatter_tokens(dot(grad_up, up_part, 0, 1))
    block_out = x3 + scatter_tokens(dot(active_bf, ffn_down_weight, 0, 0))


    sub = hidden_part // 4

    def hidden_rows(value, first):
        pieces = []
        for second in range(2):
            x, z = me_x ^ by_core(first, second), z_bit ^ by_core(second, first)
            pieces.append(rows_at(value, (2 * x + z) * sub, sub))
        return jnp.concatenate(pieces, axis=0)

    def hidden_sums(left, right):
        sent = dot(hidden_rows(left, 1), right, 1, 0).astype(BF)
        kept = dot(hidden_rows(left, 0), right, 1, 0).astype(BF)
        token = yield sent
        got = mixed(sent, in_x, in_z)
        send = plus(kept[sub:], got[sub:], token)
        own = plus(kept[:sub], got[:sub], token)
        token = yield send
        own = plus(own, mixed(send, in_z, in_x), token)
        token = yield own
        own = far_along_z(own, token)
        token = yield own
        yield own if token is None else held(own, token)

    down = hidden_sums(active_bf, cot_all)
    up_back = hidden_sums(grad_up, third_all)
    first_sent = [next(down), next(up_back)]

    def up_pair(part, token):
        blocks = part.T.reshape(n_dp, up_rows, sub)
        own = [at(blocks, me_dp)] + [dperm(at(blocks, me_dp ^ m), m) for m in range(1, n_dp)]
        own = jnp.stack(own)
        return quarter_pair(jnp.stack([at(own, me_dp ^ i) for i in range(n_dp)]), token)


    grad_three_norm = grad_three_norm + (
        gate(first_sent[0]) + gate(first_sent[1]) + gate(up_back.send(None))
    )
    back_three, ffn_gain_rows = norm_back(
        grad_three_norm, x3, three_mean, three_rstd, ffn_norm_gain, -1
    )
    grad_three = cot_rows.astype(F32) + back_three
    grad_three_bf = grad_three.astype(BF)
    grad_cross = dot(cross_out_full, grad_three_bf, 1, 1).astype(BF).reshape(H, HD, batch, length)
    grad_cprobs = jnp.einsum("hebq,bhem->bhqm", grad_cross, tv_all, preferred_element_type=F32)
    cross_dot = jnp.sum(grad_cprobs * cross_probs, axis=-1, keepdims=True)
    grad_cscores = (cross_probs * (grad_cprobs - cross_dot)).astype(BF)
    grad_cq = (
        SCALE * jnp.einsum("bhqm,bhem->hebq", grad_cscores, tk_all, preferred_element_type=F32)
    ).astype(BF)
    grad_tk = SCALE * jnp.einsum("bhqm,hebq->hbem", grad_cscores, cq, preferred_element_type=F32)
    grad_tv = jnp.einsum("bhqm,hebq->hbem", cross_probs_bf, grad_cross, preferred_element_type=F32)
    grad_tkv = jnp.concatenate([grad_tk, grad_tv], axis=2).astype(BF)
    grad_tkv = grad_tkv.reshape((n_seq // 2, 2, group_heads) + grad_tkv.shape[1:])
    tkv_keep, tkv_send = split_pair(grad_tkv, 1, me_x)
    tkv_got = xperm(tkv_send)

    sent = gate(up_back.send(grad_three_bf)) + gate(down.send(grad_three_bf))
    back_cq, cq_gain_rows = norm_back(
        grad_cq.reshape(H, HD, rows).astype(F32), cq_raw, cq_mean, cq_rstd, cq_gain + sent, -2
    )
    grad_cq_raw = back_cq.astype(BF).reshape(width, rows)
    grad_two_norm = dot(grad_cq_raw, cross_query_full, 0, 1)
    sent = gate(down.send(grad_cq_raw))
    back_two, cross_gain_rows = norm_back(
        grad_two_norm, x2, two_mean, two_rstd, cross_norm_gain + sent, -1
    )
    grad_two = grad_three + back_two
    grad_two_bf = grad_two.astype(BF)
    middle = shard_sums(
        [
            as_shards(dot(cross_tokens, grad_three_bf, 1, 0).astype(BF)),
            as_shards(dot(second_bf, grad_cq_raw, 0, 1).astype(BF)),
            as_shards(dot(self_tokens, grad_two_bf, 1, 0).astype(BF)),
        ]
    )
    next(middle)
    grad_out = dot(self_out_full, grad_two_bf, 1, 1).astype(BF)
    grad_out = to_heads(grad_out.reshape(n_seq, group_heads, 1, HD, rows))
    pin = pin_of(middle.send(grad_two_bf))
    (grad_heads,) = attention_call(
        attend_backward_kernel, [qkv, log_sum, grad_out], batch, [3], "attend_backward", pin
    )
    grad_tokens = to_tokens(grad_heads)
    middle_x = middle.send(grad_heads)
    back_qkv, qk_gain_sum = qkv_norm_call(
        grad_tokens, qkv_raw, qk_gain + gate(middle_x), tables, n_seq, "qkv_norm_back"
    )
    back_qkv = back_qkv.reshape(3 * width, rows)
    late = shard_sums([as_shards(dot(first_bf, back_qkv, 0, 1).astype(BF))])
    next(late)
    grad_one_norm = dot(back_qkv, qkv_full, 0, 1)
    middle_z = middle.send(back_qkv)
    late_far = late.send(back_qkv)
    grad_one_norm = grad_one_norm + (gate(middle_z) + gate(late_far))
    shift_part = jnp.sum(grad_one_norm.reshape(batch, length, width), axis=1)
    back_one, self_gain_rows = norm_back(
        grad_one_norm, x1, one_mean, one_rstd, self_norm_gain, -1
    )
    grad_one_bf = (grad_two + back_one).astype(BF)
    skip_blocks = dot(skip_bf, grad_one_bf, 0, 0).astype(BF)
    skip_blocks = skip_blocks.reshape(n_dp // 2, 2, 2, -1, width)
    end = shard_sums([skip_blocks[:, :, i] for i in range(2)], joined=True)
    next(end)
    grad_skip_norm = dot(grad_one_bf, skip_full, 1, 1)
    grad_tkv = plus(tkv_keep, tkv_got, grad_one_bf)
    grad_tkv = lax.psum_scatter(grad_tkv, "z", scatter_dimension=0, tiled=True)
    middle_z = middle.send(grad_one_bf)
    back_joined, skip_gain_rows = norm_back(
        grad_skip_norm, joined, skip_mean, skip_rstd, skip_gain + gate(middle_z), -1
    )

    steps = [grad_one_bf]

    def then(value):
        steps.append(value[0] if isinstance(value, list) else value)
        return value

    def step(sums):
        return then(sums.send(steps[-1]))

    step(down)
    down_own = down.send(None)
    step(end)
    step(late)
    down_pair = then(quarter_pair(down_own, steps[-1]))
    step(up_back)
    up_own = up_back.send(None)
    step(end)
    step(middle)
    step(late)
    up_grad_pair = then(up_pair(up_own, steps[-1]))
    step(end)
    step(middle)
    step(late)
    down_grad = then(quarters_in_order(down_pair, 0, steps[-1]))
    step(end)
    up_grad = then(quarters_in_order(up_grad_pair, 2, steps[-1]))
    up_grad = up_grad.transpose(1, 0, 2).reshape(up_rows, -1)
    step(late)
    cross_out_grad, cross_query_grad, self_out_grad = step(middle)
    step(end)
    step(late)
    step(end)
    (qkv_grad,) = step(late)
    (skip_grad_w,) = step(end)
    back_joined = back_joined.astype(BF).reshape(batch, length, 2 * width)


    grad_tkv = grad_tkv.reshape(grad_tkv.shape[1:]).astype(F32) + gate(steps[8])
    grad_tkv = grad_tkv.swapaxes(0, 1)
    back_tk, ck_gain_rows = norm_back(
        grad_tkv[:, :, :HD], tk_raw, tk_mean, tk_rstd, ck_gain, -2
    )
    grad_tkv_bf = jnp.concatenate([back_tk, grad_tkv[:, :, HD:]], axis=2).astype(BF)
    text_kv_grad = jnp.einsum("bmc,bhem->che", text_full, grad_tkv_bf, preferred_element_type=F32)
    text_part = jnp.einsum("bhem,che->cbm", grad_tkv_bf, text_weight, preferred_element_type=F32)
    text_part = text_part.astype(BF).reshape(n_seq // 2, 2, -1, batch * text_len)
    text_keep, text_send = split_pair(text_part, 1, me_x)
    text_part = plus(text_keep, xperm(text_send))
    text_grad = lax.psum_scatter(text_part, "z", scatter_dimension=0, tiled=True)
    text_grad = text_grad.reshape(-1, batch, text_len).transpose(1, 2, 0)
    text_kv_grad = text_kv_grad.astype(BF).reshape(n_dp // 2, 2, text_count, -1)
    text_keep, text_send = split_pair(text_kv_grad, 1, me_dp & 1)
    text_own = plus(text_keep, dperm(text_send, 1))
    text_kv_sum = at(text_own, me_dp >> 1)
    for mask in far_masks:
        text_kv_sum = plus(text_kv_sum, dperm(at(text_own, (me_dp ^ mask) >> 1), mask))
    text_kv_sum = text_kv_sum.astype(F32).reshape(text_kv_weight.shape)


    shift_slots = lax.dynamic_update_slice_in_dim(
        jnp.zeros((n_dp * batch, width), F32), shift_part, me_dp * batch, axis=0
    )
    vectors = [
        jnp.sum(ffn_gain_rows, axis=0),
        jnp.sum(cross_gain_rows, axis=0),
        jnp.sum(self_gain_rows, axis=0),
        qk_gain_sum[0, :, 0],
        qk_gain_sum[1, :, 0],
        jnp.sum(cq_gain_rows, axis=(0, 2)),
        jnp.sum(ck_gain_rows, axis=(0, 1, 3)),
        shift_slots.reshape(-1),
    ]
    vectors.append(jnp.sum(skip_gain_rows, axis=0))
    total = sum_all(jnp.concatenate(vectors))
    sums, start = [], 0
    for vector in vectors:
        sums.append(total[start : start + vector.shape[0]])
        start += vector.shape[0]
    ffn_gain, cross_gain, self_gain, q_gain_all, k_gain_all, cq_gain_sum, ck_gain_sum = sums[:7]
    shift_total, skip_gain_sum = sums[7:]
    shift_grad = lax.dot_general(
        embed_part.astype(F32),
        shift_total.reshape(n_dp * batch, width),
        (((0,), (0,)), ((), ())),
        precision=lax.Precision.HIGHEST,
        preferred_element_type=F32,
    )

    return (
        block_out.astype(BF).reshape(batch, length, width),
        back_joined[..., :width],
        back_joined[..., width:],
        text_grad,
        skip_gain_sum,
        skip_grad_w,
        self_gain,
        shift_grad,
        qkv_grad,
        q_gain_all,
        k_gain_all,
        self_out_grad,
        cross_gain,
        cross_query_grad,
        text_kv_sum,
        cq_gain_sum,
        ck_gain_sum,
        cross_out_grad,
        ffn_gain,
        up_grad,
        down_grad,
    )


def solution(mesh):
    n_dp, n_seq = mesh.shape["dp"], mesh.shape["seq"]
    mesh = Mesh(mesh.devices.reshape(n_dp, n_seq // 2, 2), ("dp", "z", "x"))
    tokens, text, rows, none = P("dp", SEQ, None), P("dp", None, SEQ), P("dp", None), P()
    heads = P("dp", SEQ, None)
    placed = (
        tokens, tokens, text, P("dp"), text, tokens, none, rows, none, rows, rows, none, none,
        rows, none, rows, heads, none, none, rows, none, rows, rows,
    )
    given = (
        tokens, tokens, tokens, text, none, rows, none, rows, rows, none, none, rows, none, rows,
        heads, none, none, rows, none, rows, rows,
    )
    return jax.shard_map(local, mesh=mesh, in_specs=placed, out_specs=given, check_vma=False)
```
